32 devices in a mesh: atoms: 8 (over y, x, core), kpt: 4 (over z).
Axes of the slice: x: 2, y: 2, z: 4, core: 2. Of those that a mesh axis runs over, the one named last changes fastest.
Arguments:
- blocks: bfloat16 [288, 32, 13, 13], P('atoms', 'kpt'), may hold values from -0.3125 to 0.3125
- vectors: bfloat16 [8, 288, 2, 13, 128], P('kpt', 'atoms'), may hold values from -6 to 6
- kvecs: float32 [8, 2], replicated, may hold values from 0 to 1
- neighbours: int32 [288, 32], P('atoms'), may hold values from 0 to 287, as said below
- offsets: int32 [288, 32], P('atoms'), may hold values from 0 to 48
- counts: int32 [288], P('atoms'), may hold values from 16 to 32
Outputs:
- first: bfloat16 [8, 288, 2, 13, 128], P('kpt', 'atoms')
- second: bfloat16 [8, 288, 2, 13, 128], P('kpt', 'atoms')
The draws below stay inside these ranges and needn't reach their ends.
Inputs may be any that keep to these rules, and one draw needn't show every extreme that they name: neighbours[a, s] = (a + d) mod 288 with -32 <= d <= 32; both d = 32 and d = -32 occur.
All inputs are finite; a program needn't handle non-finite values.
Results may differ from the reference program's by a relative error of at most 0.0063.
Values may be sent and summed in bfloat16 or wider, within the bound.
A program may use at most 128 MiB of HBM per device.

```python
import math
import jax
import jax.numpy as jnp
from jax import lax

ATOM_ORBITALS = 13
NV = 128
NEIGHBOUR_SLOTS = 32
LATTICE_OFFSETS = 49
NK = 8
NEIGHBOUR_REACH = 32
CELL_ATOMS = 288


def draw_neighbours(key, part):
    sampled_reach = jax.random.randint(key, (CELL_ATOMS, NEIGHBOUR_SLOTS), -NEIGHBOUR_REACH, NEIGHBOUR_REACH + 1)
    sampled_reach = sampled_reach.at[0, 1].set(NEIGHBOUR_REACH).at[1, 1].set(-NEIGHBOUR_REACH).at[0, 2].set(-1).at[0, 3].set(0)
    return ((jnp.arange(CELL_ATOMS, dtype=jnp.int32)[:, None] + sampled_reach) % CELL_ATOMS).astype(jnp.int32)


def draw_counts(key, part):
    sampled_neighbours = jax.random.randint(key, (CELL_ATOMS,), NEIGHBOUR_SLOTS // 2, NEIGHBOUR_SLOTS + 1)
    return sampled_neighbours.at[0].set(NEIGHBOUR_SLOTS).at[1].set(NEIGHBOUR_SLOTS // 2).astype(jnp.int32)


def touch_ends(array, key, least, top_value):
    spot = [jax.random.randint(jax.random.fold_in(key, axis), (), 0, length) for axis, length in enumerate(array.shape)]
    main_axis = array.shape.index(max(array.shape))
    neighbour = spot[:main_axis] + [(spot[main_axis] + 1) % array.shape[main_axis]] + spot[main_axis + 1:]
    return array.at[tuple(spot)].set(least).at[tuple(neighbour)].set(top_value)


def block_scale(stream_key, extent, split, smallest, high):
    def one(dim, shards_of):
        heights = jax.random.uniform(jax.random.fold_in(jax.random.fold_in(stream_key, 6), dim), (shards_of,), jnp.float32, smallest / len(split), high / len(split))
        return jnp.repeat(jnp.exp(heights), extent[dim] // shards_of).reshape((-1,) + (1,) * (len(extent) - dim - 1))

    level = one(*split[0])
    for cut in split[1:]:
        level = level * one(*cut)
    return level


def bell_draw(rng, dims, width, limit, pieces=(), held_as=jnp.bfloat16):
    loudness = block_scale(rng, dims, pieces, -0.22, 0.18) if pieces else 1.0
    entries = jax.random.normal(rng, dims, jnp.float32) * width * loudness
    return jnp.minimum(jnp.maximum(entries, -limit), limit).astype(held_as)


def setup_inputs(seed: int = 0) -> dict:
    key_list = jax.random.split(jax.random.key(seed), 7)
    return {
        "blocks": bell_draw(key_list[0], (CELL_ATOMS, NEIGHBOUR_SLOTS, ATOM_ORBITALS, ATOM_ORBITALS), (ATOM_ORBITALS * NEIGHBOUR_SLOTS) ** -0.5, 0.3125, ((0, 8), (1, 4))),
        "vectors": bell_draw(key_list[1], (NK, CELL_ATOMS, 2, ATOM_ORBITALS, NV), 1.0, 6.0, ((0, 4), (1, 8))),
        "kvecs": jnp.clip(jax.random.uniform(key_list[2], (NK, 2), jnp.float32, 0.0, 1.0), 0.0, 1.0),
        "neighbours": draw_neighbours(jax.random.fold_in(key_list[6], 71), 0),
        "offsets": touch_ends(jax.random.randint(key_list[4], (CELL_ATOMS, NEIGHBOUR_SLOTS), 0, LATTICE_OFFSETS), jax.random.fold_in(key_list[4], 1), 0, LATTICE_OFFSETS - 1).astype(jnp.int32),
        "counts": draw_counts(jax.random.fold_in(key_list[6], 71), 0),
    }


def angles(kvecs, offsets):
    grid_row = (offsets // 7 - 3).astype(jnp.float32)
    grid_col = (offsets % 7 - 3).astype(jnp.float32)
    return 2.0 * math.pi * (kvecs[:, 0, None, None] * grid_row[None] + kvecs[:, 1, None, None] * grid_col[None])


def phased(kvecs, offsets, counts, blocks):
    theta = angles(kvecs, offsets)
    live_slot = jnp.arange(offsets.shape[1], dtype=jnp.int32)[None, :] < counts[:, None]
    block_f = blocks.astype(jnp.float32)[None]
    cos_part = jnp.where(live_slot[None], jnp.cos(theta), 0.0)[..., None, None]
    sin_part = jnp.where(live_slot[None], jnp.sin(theta), 0.0)[..., None, None]
    return (cos_part * block_f).astype(jnp.bfloat16), (sin_part * block_f).astype(jnp.bfloat16)


def apply_one(real_h, imag_h, vector_k, neighbours):
    def take_slot(running, slot_index):
        picked = vector_k[neighbours[:, slot_index]].astype(jnp.float32)
        real_s = real_h[:, slot_index].astype(jnp.float32)
        imag_s = imag_h[:, slot_index].astype(jnp.float32)
        real_out = jnp.einsum('aop,apv->aov', real_s, picked[:, 0]) - jnp.einsum('aop,apv->aov', imag_s, picked[:, 1])
        imag_out = jnp.einsum('aop,apv->aov', real_s, picked[:, 1]) + jnp.einsum('aop,apv->aov', imag_s, picked[:, 0])
        return running + jnp.stack([real_out, imag_out], axis=1), None
    start_sum = jnp.zeros(vector_k.shape, jnp.float32)
    summed, unused = lax.scan(take_slot, start_sum, jnp.arange(neighbours.shape[1], dtype=jnp.int32))
    return summed.astype(jnp.bfloat16)


def reference(blocks, vectors, kvecs, neighbours, offsets, counts):
    def per_point(packed):
        kvec_one, vector_k = packed
        real_h, imag_h = phased(kvec_one[None], offsets, counts, blocks)
        first_k = apply_one(real_h[0], imag_h[0], vector_k, neighbours)
        second_k = apply_one(real_h[0], imag_h[0], first_k, neighbours)
        return first_k, second_k
    first, second = lax.map(per_point, (kvecs, vectors))
    return (first, second)
```

```python
import functools
import math

import jax
import jax.numpy as jnp
from jax import lax
from jax.experimental import pallas as pl
from jax.experimental.pallas import tpu as pltpu
from jax.sharding import PartitionSpec as P

REACH = 32
ORB = 16
LANES = 128
OWN = 48
LEFT = OWN
RIGHT = OWN + REACH
CHUNKS = 3
MESH = pl.DeviceIdType.MESH


def kernel(
    n_atoms, n_kpt, blk, vec, tab, first, second,
    gather, ham, win, win2, send_r, send_r2, rows, prod, hot,
    blk_send, blk_recv, halo_send, halo_recv, own_sem,
):
    points, atoms, _, orbitals, _ = vec.shape
    pairs = atoms // 2
    me = lax.axis_index("atoms")
    z = lax.axis_index("kpt")
    left, right = lax.rem(me + n_atoms - 1, n_atoms), lax.rem(me + 1, n_atoms)
    others = [lax.rem(z + d, n_kpt) for d in range(1, n_kpt)]

    barrier = pltpu.get_barrier_semaphore()
    for peer in (left, right):
        pl.semaphore_signal(barrier, inc=1, device_id=(peer, z), device_id_type=MESH)
    for other in others:
        pl.semaphore_signal(barrier, inc=1, device_id=(me, other), device_id_type=MESH)
    pl.semaphore_wait(barrier, 2 + len(others))

    chunk_rows = blk.shape[0] // CHUNKS

    def block_copy(c, d, slab, other):
        part = pl.ds(c * chunk_rows, chunk_rows)
        return pltpu.make_async_remote_copy(
            src_ref=blk.at[part],
            dst_ref=gather.at[slab, part],
            send_sem=blk_send.at[c, d],
            recv_sem=blk_recv.at[c, slab],
            device_id=(me, other),
            device_id_type=MESH,
        )

    own_copy = pltpu.make_async_copy(blk, gather.at[z], own_sem)
    own_copy.start()
    for c in range(CHUNKS):
        for d, other in enumerate(others):
            block_copy(c, d, z, other).start()

    def halo_copies(step, k, window, to_right):
        return (
            pltpu.make_async_remote_copy(
                src_ref=to_right.at[k],
                dst_ref=window.at[k, :, pl.ds(LEFT, REACH)],
                send_sem=halo_send.at[step, k, 0],
                recv_sem=halo_recv.at[step, k, 0],
                device_id=(right, z),
                device_id_type=MESH,
            ),
            pltpu.make_async_remote_copy(
                src_ref=window.at[k, :, pl.ds(0, REACH)],
                dst_ref=window.at[k, :, pl.ds(RIGHT, REACH)],
                send_sem=halo_send.at[step, k, 1],
                recv_sem=halo_recv.at[step, k, 1],
                device_id=(left, z),
                device_id_type=MESH,
            ),
        )

    def fill_window(k, window, to_right):
        for p in range(orbitals):
            for c in range(2):
                lanes = pl.ds(c * LANES, LANES)
                own = rows[c, pl.ds(p, OWN, stride=ORB), :]
                window[k, p, 0:OWN, lanes] = own.astype(jnp.bfloat16)
                tail = rows[c, pl.ds(p + (atoms - REACH) * ORB, REACH, stride=ORB), :]
                to_right[k, p, :, lanes] = tail.astype(jnp.bfloat16)

    rows[...] = jnp.zeros_like(rows)
    spare = pl.ds(RIGHT + REACH, LANES - RIGHT - REACH)
    for window in (win, win2):
        window[:, :, spare, :] = jnp.zeros(
            (points, orbitals, LANES - RIGHT - REACH, 2 * LANES), jnp.bfloat16
        )
    for k in range(points):
        for a in range(atoms):
            for c in range(2):
                rows[c, a * ORB : a * ORB + orbitals, :] = vec[k, a, c].astype(jnp.float32)
        fill_window(k, win, send_r)
        for copy in halo_copies(0, k, win, send_r):
            copy.start()

    own_copy.wait()
    lane = lax.broadcasted_iota(jnp.int32, (n_kpt * 16, LANES), 1).astype(jnp.float32)
    depth = n_kpt * 16

    def build(pair, carry):
        at = pl.multiple_of(pair * 16, 16)
        held = [gather[s, pl.ds(at, 16), :] for s in range(n_kpt)]
        flipped = jnp.concatenate(held + held, axis=0).T[: orbitals * ORB]
        cols = tab[pl.ds(pl.multiple_of(pair * depth, depth), depth), :]
        place = jnp.broadcast_to(cols[:, 0:1], (depth, LANES))
        phases = [
            jnp.broadcast_to(cols[:, 1 + j : 2 + j], (depth, LANES)) for j in range(2 * points)
        ]
        for a in range(2):
            hit = place == lane + float(a * LANES)
            for k in range(points):
                for c in range(2):
                    value = jnp.where(hit, phases[2 * k + c], 0.0)
                    high = value.astype(jnp.bfloat16)
                    low = (value - high.astype(jnp.float32)).astype(jnp.bfloat16)
                    lanes = pl.ds(c * LANES, LANES)
                    hot[a, k, 0:depth, lanes] = high
                    hot[a, k, depth : 2 * depth, lanes] = low
        for a in range(2):
            for k in range(points):
                dense = jnp.dot(
                    flipped, hot[a, k], preferred_element_type=jnp.float32
                ).astype(jnp.bfloat16)
                for c in range(2):
                    base = pl.multiple_of(c * atoms * ORB + pair * 2 * ORB + a * ORB, ORB)
                    for p in range(orbitals):
                        ham[k, pl.ds(base, ORB), p * LANES : (p + 1) * LANES] = dense[
                            p * ORB : (p + 1) * ORB, c * LANES : (c + 1) * LANES
                        ]
        return carry

    for c in range(CHUNKS):
        for other in others:
            block_copy(c, 0, other, other).wait_recv()
        lax.fori_loop(c * pairs // CHUNKS, (c + 1) * pairs // CHUNKS, build, 0)

    half = atoms * ORB

    def apply(k, window, out):
        prod[...] = jnp.dot(
            ham[k],
            window[k].reshape(orbitals * LANES, 2 * LANES),
            preferred_element_type=jnp.float32,
        )
        real = prod[0:half, 0:LANES] - prod[half : 2 * half, LANES : 2 * LANES]
        imag = prod[0:half, LANES : 2 * LANES] + prod[half : 2 * half, 0:LANES]
        for c, value in enumerate((real, imag)):
            rounded = value.astype(jnp.bfloat16).reshape(atoms, ORB, LANES)
            out[k, :, c] = rounded[:, :orbitals]
            if out is first:
                rows[c, 0:half, :] = value

    for k in range(points):
        for copy in halo_copies(0, k, win, send_r):
            copy.wait_recv()
        apply(k, win, first)
        fill_window(k, win2, send_r2)
        for copy in halo_copies(1, k, win2, send_r2):
            copy.start()
    for k in range(points):
        for copy in halo_copies(1, k, win2, send_r2):
            copy.wait_recv()
        apply(k, win2, second)

    for c in range(CHUNKS):
        for d, other in enumerate(others):
            block_copy(c, d, z, other).wait_send()
    for k in range(points):
        for copy in halo_copies(0, k, win, send_r) + halo_copies(1, k, win2, send_r2):
            copy.wait_send()


def table(kvecs, neighbours, offsets, counts):
    atoms, slots = offsets.shape
    points = kvecs.shape[0]
    total = atoms * lax.axis_size("atoms")
    row = jnp.arange(atoms, dtype=jnp.int32)[:, None]
    distance = neighbours - (lax.axis_index("atoms") * atoms + row)
    distance = (distance + total // 2) % total - total // 2
    local = row + distance
    place = jnp.where(
        local < 0, local + REACH + LEFT, jnp.where(local >= atoms, local - atoms + RIGHT, local)
    )
    place = place + LANES * (row % 2)
    live = jnp.arange(slots, dtype=jnp.int32)[None, :] < counts[:, None]
    grid_row = (offsets // 7 - 3).astype(jnp.float32)
    grid_col = (offsets % 7 - 3).astype(jnp.float32)
    columns = [place.astype(jnp.float32)]
    for k in range(points):
        theta = 2.0 * math.pi * (kvecs[k, 0] * grid_row + kvecs[k, 1] * grid_col)
        columns += [jnp.where(live, jnp.cos(theta), 0.0), jnp.where(live, jnp.sin(theta), 0.0)]
    columns += [jnp.zeros_like(columns[0])] * (8 - len(columns))
    wide = jnp.stack(columns, axis=-1)
    eight = slots // lax.axis_size("kpt")
    wide = wide.reshape(atoms // 2, 2, slots // eight, eight, 8).transpose(0, 2, 1, 3, 4)
    return wide.reshape(atoms * slots, 8)


def per_device(blocks, vectors, kvecs, neighbours, offsets, counts):
    n_atoms, n_kpt = lax.axis_size("atoms"), lax.axis_size("kpt")
    atoms, slots, orbitals, _ = blocks.shape
    points = vectors.shape[0]
    own_kvecs = lax.dynamic_slice_in_dim(kvecs, lax.axis_index("kpt") * points, points, 0)
    tab = table(own_kvecs, neighbours, offsets, counts)
    blk = jnp.pad(blocks.transpose(0, 1, 3, 2), ((0, 0), (0, 0), (0, 0), (0, ORB - orbitals)))
    blk = blk.reshape(atoms * slots, orbitals * ORB)
    blk = jnp.pad(blk, ((0, 0), (0, 2 * LANES - orbitals * ORB)))
    depth = orbitals * LANES
    bf16, f32 = jnp.bfloat16, jnp.float32
    vmem = pl.BlockSpec(memory_space=pltpu.VMEM)
    flops = 2 * points * 2 * 2 * atoms * ORB * depth * 2 * LANES
    return pl.pallas_call(
        functools.partial(kernel, n_atoms, n_kpt),
        out_shape=[jax.ShapeDtypeStruct(vectors.shape, bf16)] * 2,
        in_specs=[vmem] * 3,
        out_specs=[vmem] * 2,
        scratch_shapes=[
            pltpu.VMEM((n_kpt,) + blk.shape, bf16),
            pltpu.VMEM((points, 2 * atoms * ORB, depth), bf16),
            pltpu.VMEM((points, orbitals, LANES, 2 * LANES), bf16),
            pltpu.VMEM((points, orbitals, LANES, 2 * LANES), bf16),
            pltpu.VMEM((points, orbitals, REACH, 2 * LANES), bf16),
            pltpu.VMEM((points, orbitals, REACH, 2 * LANES), bf16),
            pltpu.VMEM((2, OWN * ORB, LANES), f32),
            pltpu.VMEM((2 * atoms * ORB, 2 * LANES), f32),
            pltpu.VMEM((2, points, 2 * 16 * n_kpt, 2 * LANES), bf16),
            pltpu.SemaphoreType.DMA((CHUNKS, n_kpt - 1)),
            pltpu.SemaphoreType.DMA((CHUNKS, n_kpt)),
            pltpu.SemaphoreType.DMA((2, points, 2)),
            pltpu.SemaphoreType.DMA((2, points, 2)),
            pltpu.SemaphoreType.DMA,
        ],
        compiler_params=pltpu.CompilerParams(
            collective_id=0, has_side_effects=True, vmem_limit_bytes=48 * 1024 * 1024
        ),
        cost_estimate=pl.CostEstimate(flops=flops, bytes_accessed=4 << 20, transcendentals=0),
    )(blk, vectors, tab)


def solution(mesh):
    placed = (
        P("atoms", "kpt", None, None),
        P("kpt", "atoms", None, None, None),
        P(),
        P("atoms", None),
        P("atoms", None),
        P("atoms"),
    )
    return jax.shard_map(
        per_device,
        mesh=mesh,
        in_specs=placed,
        out_specs=(P("kpt", "atoms", None, None, None), P("kpt", "atoms", None, None, None)),
        check_vma=False,
    )
```

```python
import functools
import math

import jax
import jax.numpy as jnp
from jax import lax
from jax.experimental import pallas as pl
from jax.experimental.pallas import tpu as pltpu
from jax.sharding import PartitionSpec as P

REACH = 32
ORB = 16
LANES = 128
OWN = 48
LEFT = OWN
RIGHT = OWN + REACH
CHUNKS = 3
MESH = pl.DeviceIdType.MESH


def kernel(
    n_atoms, n_kpt, blk, vec, near, shift, count, kvecs, first, second,
    gather, ham, win, win2, send_r, send_r2, rows, prod, hot, spread, tiles, flat,
    blk_send, blk_recv, halo_send, halo_recv,
):
    points = vec.shape[0]
    orbitals, _, eight, atoms = blk.shape
    slots = near.shape[0]
    pairs = atoms // 2
    pitch = 2 * orbitals
    me = lax.axis_index("atoms")
    z = lax.axis_index("kpt")
    left, right = lax.rem(me + n_atoms - 1, n_atoms), lax.rem(me + 1, n_atoms)
    others = [lax.rem(z + d, n_kpt) for d in range(1, n_kpt)]

    barrier = pltpu.get_barrier_semaphore()
    for peer in (left, right):
        pl.semaphore_signal(barrier, inc=1, device_id=(peer, z), device_id_type=MESH)
    for other in others:
        pl.semaphore_signal(barrier, inc=1, device_id=(me, other), device_id_type=MESH)

    chunk_rows = gather.shape[1] // CHUNKS

    def block_copy(c, d, slab, other):
        part = pl.ds(c * chunk_rows, chunk_rows)
        return pltpu.make_async_remote_copy(
            src_ref=gather.at[slab, part],
            dst_ref=gather.at[slab, part],
            send_sem=blk_send.at[c, d],
            recv_sem=blk_recv.at[c, slab],
            device_id=(me, other),
            device_id_type=MESH,
        )

    def halo_copies(step, k, window, to_right):
        return (
            pltpu.make_async_remote_copy(
                src_ref=to_right.at[k],
                dst_ref=window.at[k, :, pl.ds(LEFT, REACH)],
                send_sem=halo_send.at[step, k, 0],
                recv_sem=halo_recv.at[step, k, 0],
                device_id=(right, z),
                device_id_type=MESH,
            ),
            pltpu.make_async_remote_copy(
                src_ref=window.at[k, :, pl.ds(0, REACH)],
                dst_ref=window.at[k, :, pl.ds(RIGHT, REACH)],
                send_sem=halo_send.at[step, k, 1],
                recv_sem=halo_recv.at[step, k, 1],
                device_id=(left, z),
                device_id_type=MESH,
            ),
        )

    def fill_window(k, window, to_right):
        for p in range(orbitals):
            for c in range(2):
                lanes = pl.ds(c * LANES, LANES)
                own = rows[pl.ds(2 * p + c, OWN, stride=pitch), :]
                window[k, p, 0:OWN, lanes] = own.astype(jnp.bfloat16)
                tail = rows[pl.ds(2 * p + c + (atoms - REACH) * pitch, REACH, stride=pitch), :]
                to_right[k, p, :, lanes] = tail.astype(jnp.bfloat16)

    rows[atoms * pitch :, :] = jnp.zeros(((OWN - atoms) * pitch, LANES), jnp.float32)
    for k in range(points):
        rows[0 : atoms * pitch, :] = vec[k].astype(jnp.float32)
        fill_window(k, win, send_r)
        if k == 0:
            pl.semaphore_wait(barrier, 2 + len(others))
        for copy in halo_copies(0, k, win, send_r):
            copy.start()

    for p in range(orbitals):
        for o in range(ORB):
            at = (p * ORB + o) * eight
            if o < orbitals:
                tiles[at : at + eight, 0:atoms] = blk[o, p].astype(jnp.float32)
            else:
                tiles[at : at + eight, :] = jnp.zeros((eight, LANES), jnp.float32)
    used = orbitals * ORB
    for s in range(eight):
        one = tiles[pl.ds(s, used, stride=eight), :]
        one = jnp.concatenate([one, jnp.zeros((2 * LANES - used, LANES), jnp.float32)], axis=0)
        for half_lanes in range(2):
            turned = one[half_lanes * LANES : (half_lanes + 1) * LANES].T
            flat[half_lanes, pl.ds(s, atoms, stride=eight), :] = turned[:atoms]
    for half_lanes in range(2):
        gather[z, :, half_lanes * LANES : (half_lanes + 1) * LANES] = flat[half_lanes].astype(
            jnp.bfloat16
        )
    for c in range(CHUNKS):
        for d, other in enumerate(others):
            block_copy(c, d, z, other).start()

    spare = pl.ds(RIGHT + REACH, LANES - RIGHT - REACH)
    for window in (win, win2):
        window[:, :, spare, :] = jnp.zeros(
            (points, orbitals, LANES - RIGHT - REACH, 2 * LANES), jnp.bfloat16
        )

    total = atoms * n_atoms
    row = lax.broadcasted_iota(jnp.int32, (slots, atoms), 1)
    distance = near[...] - (me * atoms + row)
    distance = jnp.where(distance > total // 2, distance - total, distance)
    distance = jnp.where(distance < -(total // 2), distance + total, distance)
    local = row + distance
    place = jnp.where(
        local < 0, local + REACH + LEFT, jnp.where(local >= atoms, local - atoms + RIGHT, local)
    )
    live = lax.broadcasted_iota(jnp.int32, (slots, atoms), 0) < count[...]
    offset = shift[...].astype(jnp.float32)
    grid_row = jnp.floor((offset + 0.5) * (1.0 / 7.0))
    grid_col = offset - 7.0 * grid_row - 3.0
    grid_row = grid_row - 3.0
    columns = [place.astype(jnp.float32)]
    for k in range(points):
        at = z * points + k
        turns = kvecs[at, 0] * grid_row + kvecs[at, 1] * grid_col
        theta = (2.0 * math.pi) * (turns - jnp.floor(turns + 0.5))
        columns += [jnp.where(live, jnp.cos(theta), 0.0), jnp.where(live, jnp.sin(theta), 0.0)]
    for a in range(atoms):
        for j, column in enumerate(columns):
            spread[a, j] = jnp.broadcast_to(column[:, a : a + 1], (slots, LANES))

    lane = lax.broadcasted_iota(jnp.int32, (slots, LANES), 1).astype(jnp.float32)
    depth = 2 * slots
    nothing = jnp.zeros((eight, LANES), jnp.float32)

    def heat(pair, carry):
        for a in range(2):
            atom = 2 * pair + a
            hit = spread[atom, 0] == lane
            for k in range(points):
                for c in range(2):
                    value = jnp.where(hit, spread[atom, 1 + 2 * k + c], 0.0)
                    high = value.astype(jnp.bfloat16).astype(jnp.float32)
                    for part, piece in enumerate((high, value - high)):
                        laid = []
                        for s in range(n_kpt):
                            mine = piece[s * eight : (s + 1) * eight]
                            laid += [nothing, mine] if a else [mine, nothing]
                        hot[atom, k, part * depth : (part + 1) * depth,
                            c * LANES : (c + 1) * LANES] = jnp.concatenate(
                            laid, axis=0
                        ).astype(jnp.bfloat16)
        return carry

    lax.fori_loop(0, pairs, heat, 0)

    def build(pair, carry):
        at = pl.multiple_of(pair * 16, 16)
        held = [gather[s, pl.ds(at, 16), :] for s in range(n_kpt)]
        flipped = jnp.concatenate(held + held, axis=0).T[:used]
        for a in range(2):
            for k in range(points):
                dense = jnp.dot(
                    flipped, hot[2 * pair + a, k], preferred_element_type=jnp.float32
                ).astype(jnp.bfloat16)
                for c in range(2):
                    base = pl.multiple_of(c * atoms * ORB + pair * 2 * ORB + a * ORB, ORB)
                    for p in range(orbitals):
                        ham[k, pl.ds(base, ORB), p * LANES : (p + 1) * LANES] = dense[
                            p * ORB : (p + 1) * ORB, c * LANES : (c + 1) * LANES
                        ]
        return carry

    for c in range(CHUNKS):
        for other in others:
            block_copy(c, 0, other, other).wait_recv()
        lax.fori_loop(c * pairs // CHUNKS, (c + 1) * pairs // CHUNKS, build, 0)

    half = atoms * ORB

    def apply(k, window, out):
        prod[...] = jnp.dot(
            ham[k],
            window[k].reshape(orbitals * LANES, 2 * LANES),
            preferred_element_type=jnp.float32,
        )
        real = prod[0:half, 0:LANES] - prod[half : 2 * half, LANES : 2 * LANES]
        imag = prod[0:half, LANES : 2 * LANES] + prod[half : 2 * half, 0:LANES]
        for c, value in enumerate((real, imag)):
            for a in range(atoms):
                rows[pl.ds(a * pitch + c, orbitals, stride=2), :] = value[
                    a * ORB : a * ORB + orbitals
                ]
        out[k] = rows[0 : atoms * pitch, :].astype(jnp.bfloat16)

    for k in range(points):
        for copy in halo_copies(0, k, win, send_r):
            copy.wait_recv()
        apply(k, win, first)
        fill_window(k, win2, send_r2)
        for copy in halo_copies(1, k, win2, send_r2):
            copy.start()
    for k in range(points):
        for copy in halo_copies(1, k, win2, send_r2):
            copy.wait_recv()
        apply(k, win2, second)

    for c in range(CHUNKS):
        for d, other in enumerate(others):
            block_copy(c, d, z, other).wait_send()
    for k in range(points):
        for copy in halo_copies(0, k, win, send_r) + halo_copies(1, k, win2, send_r2):
            copy.wait_send()


def per_device(blocks, vectors, kvecs, neighbours, offsets, counts):
    n_atoms, n_kpt = lax.axis_size("atoms"), lax.axis_size("kpt")
    atoms, eight, orbitals, _ = blocks.shape
    slots = neighbours.shape[1]
    points = vectors.shape[0]
    flat_vectors = vectors.transpose(0, 1, 3, 2, 4).reshape(points, atoms * 2 * orbitals, LANES)
    depth = orbitals * LANES
    bf16, f32 = jnp.bfloat16, jnp.float32
    vmem = pl.BlockSpec(memory_space=pltpu.VMEM)
    smem = pl.BlockSpec(memory_space=pltpu.SMEM)
    flops = 2 * points * 2 * 2 * atoms * ORB * depth * 2 * LANES
    outs = pl.pallas_call(
        functools.partial(kernel, n_atoms, n_kpt),
        out_shape=[jax.ShapeDtypeStruct(flat_vectors.shape, bf16)] * 2,
        in_specs=[vmem] * 5 + [smem],
        out_specs=[vmem] * 2,
        scratch_shapes=[
            pltpu.VMEM((n_kpt, atoms * eight, 2 * LANES), bf16),
            pltpu.VMEM((points, 2 * atoms * ORB, depth), bf16),
            pltpu.VMEM((points, orbitals, LANES, 2 * LANES), bf16),
            pltpu.VMEM((points, orbitals, LANES, 2 * LANES), bf16),
            pltpu.VMEM((points, orbitals, REACH, 2 * LANES), bf16),
            pltpu.VMEM((points, orbitals, REACH, 2 * LANES), bf16),
            pltpu.VMEM((OWN * 2 * orbitals, LANES), f32),
            pltpu.VMEM((2 * atoms * ORB, 2 * LANES), f32),
            pltpu.VMEM((atoms, points, 4 * slots, 2 * LANES), bf16),
            pltpu.VMEM((atoms, 1 + 2 * points, slots, LANES), f32),
            pltpu.VMEM((orbitals * ORB * eight, LANES), f32),
            pltpu.VMEM((2, atoms * eight, LANES), f32),
            pltpu.SemaphoreType.DMA((CHUNKS, n_kpt - 1)),
            pltpu.SemaphoreType.DMA((CHUNKS, n_kpt)),
            pltpu.SemaphoreType.DMA((2, points, 2)),
            pltpu.SemaphoreType.DMA((2, points, 2)),
        ],
        compiler_params=pltpu.CompilerParams(
            collective_id=0, has_side_effects=True, vmem_limit_bytes=48 * 1024 * 1024
        ),
        cost_estimate=pl.CostEstimate(flops=flops, bytes_accessed=4 << 20, transcendentals=0),
    )(
        blocks.transpose(2, 3, 1, 0), flat_vectors, neighbours.T, offsets.T, counts[None, :], kvecs
    )
    return tuple(
        out.reshape(points, atoms, orbitals, 2, LANES).transpose(0, 1, 3, 2, 4) for out in outs
    )


def solution(mesh):
    placed = (
        P("atoms", "kpt", None, None),
        P("kpt", "atoms", None, None, None),
        P(),
        P("atoms", None),
        P("atoms", None),
        P("atoms"),
    )
    return jax.shard_map(
        per_device,
        mesh=mesh,
        in_specs=placed,
        out_specs=(P("kpt", "atoms", None, None, None), P("kpt", "atoms", None, None, None)),
        check_vma=False,
    )
```

```python
import functools
import math

import jax
import jax.numpy as jnp
from jax import lax
from jax.experimental import pallas as pl
from jax.experimental.pallas import tpu as pltpu
from jax.sharding import PartitionSpec as P

REACH = 32
ORB = 16
LANES = 128
OWN = 48
LEFT = OWN
RIGHT = OWN + REACH
CHUNKS = 3
WIDE = 9
PACK = 14
MESH = pl.DeviceIdType.MESH


def kernel(
    n_atoms, n_kpt, blk_hbm, vec_hbm, near_hbm, shift_hbm, count_hbm, kvecs_hbm, first, second,
    blk, vec, near, shift, count, kvecs,
    gather, ham, win, win2, send_r, send_r2, rows, prod, hot, spread, tiles, flat, turn, made,
    blk_send, blk_recv, halo_send, halo_recv, load_sem, store_sem,
):
    loads = [
        pltpu.make_async_copy(source, held, load_sem.at[i])
        for i, (source, held) in enumerate(
            (
                (vec_hbm, vec), (blk_hbm, blk), (near_hbm, near),
                (shift_hbm, shift), (count_hbm, count), (kvecs_hbm, kvecs),
            )
        )
    ]
    for load in loads:
        load.start()
    points = vec.shape[0]
    orbitals, _, eight, atoms = blk.shape
    slots = near.shape[0]
    pairs = atoms // 2
    pitch = 2 * orbitals
    me = lax.axis_index("atoms")
    z = lax.axis_index("kpt")
    left, right = lax.rem(me + n_atoms - 1, n_atoms), lax.rem(me + 1, n_atoms)
    others = [lax.rem(z + d, n_kpt) for d in range(1, n_kpt)]

    barrier = pltpu.get_barrier_semaphore()
    for peer in (left, right):
        pl.semaphore_signal(barrier, inc=1, device_id=(peer, z), device_id_type=MESH)
    for other in others:
        pl.semaphore_signal(barrier, inc=1, device_id=(me, other), device_id_type=MESH)

    chunk_rows = gather.shape[1] // CHUNKS

    def block_copy(c, d, slab, other):
        part = pl.ds(c * chunk_rows, chunk_rows)
        return pltpu.make_async_remote_copy(
            src_ref=gather.at[slab, part],
            dst_ref=gather.at[slab, part],
            send_sem=blk_send.at[c, d],
            recv_sem=blk_recv.at[c, slab],
            device_id=(me, other),
            device_id_type=MESH,
        )

    def halo_copies(step, k, window, to_right):
        return (
            pltpu.make_async_remote_copy(
                src_ref=to_right.at[k],
                dst_ref=window.at[k, :, pl.ds(LEFT, REACH)],
                send_sem=halo_send.at[step, k, 0],
                recv_sem=halo_recv.at[step, k, 0],
                device_id=(right, z),
                device_id_type=MESH,
            ),
            pltpu.make_async_remote_copy(
                src_ref=window.at[k, :, pl.ds(0, REACH)],
                dst_ref=window.at[k, :, pl.ds(RIGHT, REACH)],
                send_sem=halo_send.at[step, k, 1],
                recv_sem=halo_recv.at[step, k, 1],
                device_id=(left, z),
                device_id_type=MESH,
            ),
        )

    def fill_window(k, window, to_right):
        for p in range(orbitals):
            for c in range(2):
                lanes = pl.ds(c * LANES, LANES)
                own = rows[pl.ds(2 * p + c, OWN, stride=pitch), :]
                window[k, p, 0:OWN, lanes] = own.astype(jnp.bfloat16)
                tail = rows[pl.ds(2 * p + c + (atoms - REACH) * pitch, REACH, stride=pitch), :]
                to_right[k, p, :, lanes] = tail.astype(jnp.bfloat16)

    rows[atoms * pitch :, :] = jnp.zeros(((OWN - atoms) * pitch, LANES), jnp.float32)
    for p in range(WIDE):
        at = (p * PACK + orbitals) * eight
        tiles[at : at + eight, :] = jnp.zeros((eight, LANES), jnp.float32)
    tiles[WIDE * PACK * eight : LANES * eight, :] = jnp.zeros(
        ((LANES - WIDE * PACK) * eight, LANES), jnp.float32
    )
    for p in range(orbitals - WIDE):
        at = (LANES + p * ORB + orbitals) * eight
        tiles[at : at + (ORB - orbitals) * eight, :] = jnp.zeros(
            ((ORB - orbitals) * eight, LANES), jnp.float32
        )

    def send_vectors(k):
        rows[0 : atoms * pitch, :] = vec[k].astype(jnp.float32)
        fill_window(k, win, send_r)
        if k == 0:
            pl.semaphore_wait(barrier, 2 + len(others))
        for copy in halo_copies(0, k, win, send_r):
            copy.start()

    loads[0].wait()
    send_vectors(0)

    loads[1].wait()
    for p in range(orbitals):
        for o in range(orbitals):
            at = p * PACK + o if p < WIDE else LANES + (p - WIDE) * ORB + o
            tiles[at * eight : (at + 1) * eight, 0:atoms] = blk[o, p].astype(jnp.float32)
    narrow = LANES // 2
    for s in range(eight):
        wide = tiles[pl.ds(s, LANES, stride=eight), :]
        rest = tiles[pl.ds(LANES * eight + s, narrow, stride=eight), :]
        flat[0, pl.ds(s, atoms, stride=eight), :] = wide.T[:atoms]
        rest = jnp.concatenate([rest, rest], axis=0)
        flat[1, pl.ds(s, atoms, stride=eight), :] = rest.T[:atoms]
    even_side = lax.broadcasted_iota(jnp.int32, (16, LANES), 1) < narrow
    for quad in range(atoms // 4):
        at, to = quad * 32, quad * 48
        gather[z, to : to + 32] = flat[0, at : at + 32].astype(jnp.bfloat16)
        gather[z, to + 32 : to + 48] = jnp.where(
            even_side, flat[1, at : at + 16], flat[1, at + 16 : at + 32]
        ).astype(jnp.bfloat16)
    for c in range(CHUNKS):
        for d, other in enumerate(others):
            block_copy(c, d, z, other).start()
    for k in range(1, points):
        send_vectors(k)

    spare = pl.ds(RIGHT + REACH, LANES - RIGHT - REACH)
    for window in (win, win2):
        window[:, :, spare, :] = jnp.zeros(
            (points, orbitals, LANES - RIGHT - REACH, 2 * LANES), jnp.bfloat16
        )

    for load in loads[2:]:
        load.wait()
    total = atoms * n_atoms
    row = lax.broadcasted_iota(jnp.int32, (slots, atoms), 1)
    distance = near[...] - (me * atoms + row)
    distance = jnp.where(distance > total // 2, distance - total, distance)
    distance = jnp.where(distance < -(total // 2), distance + total, distance)
    local = row + distance
    place = jnp.where(
        local < 0, local + REACH + LEFT, jnp.where(local >= atoms, local - atoms + RIGHT, local)
    )
    live = lax.broadcasted_iota(jnp.int32, (slots, atoms), 0) < count[...]
    offset = shift[...].astype(jnp.float32)
    grid_row = jnp.floor((offset + 0.5) * (1.0 / 7.0))
    grid_col = offset - 7.0 * grid_row - 3.0
    grid_row = grid_row - 3.0
    columns = [place.astype(jnp.float32)]
    for k in range(points):
        own = lax.broadcasted_iota(jnp.int32, kvecs.shape, 1) == z * points + k
        kvec = jnp.sum(jnp.where(own, kvecs[...], 0.0), axis=1, keepdims=True)
        turns = kvec[0:1] * grid_row + kvec[1:2] * grid_col
        theta = (2.0 * math.pi) * (turns - jnp.floor(turns + 0.5))
        columns += [jnp.where(live, jnp.cos(theta), 0.0), jnp.where(live, jnp.sin(theta), 0.0)]
    for a in range(atoms):
        for j, column in enumerate(columns):
            spread[a, j] = jnp.broadcast_to(column[:, a : a + 1], (slots, LANES))

    lane = lax.broadcasted_iota(jnp.int32, (slots, LANES), 1).astype(jnp.float32)
    depth = 2 * slots
    nothing = jnp.zeros((eight, LANES), jnp.float32)

    def heat(pair, carry):
        for a in range(2):
            atom = 2 * pair + a
            hit = spread[atom, 0] == lane
            for k in range(points):
                for c in range(2):
                    value = jnp.where(hit, spread[atom, 1 + 2 * k + c], 0.0)
                    high = value.astype(jnp.bfloat16).astype(jnp.float32)
                    for part, piece in enumerate((high, value - high)):
                        laid = []
                        for s in range(n_kpt):
                            mine = piece[s * eight : (s + 1) * eight]
                            laid += [nothing, mine] if a else [mine, nothing]
                        hot[atom, k, part * depth : (part + 1) * depth,
                            c * LANES : (c + 1) * LANES] = jnp.concatenate(
                            laid, axis=0
                        ).astype(jnp.bfloat16)
        return carry

    lax.fori_loop(0, pairs, heat, 0)

    def build(quad, carry):
        at = pl.multiple_of(quad * 48, 16)
        for part in range(3):
            held = [gather[s, pl.ds(at + part * 16, 16), :] for s in range(n_kpt)]
            turn[part] = jnp.concatenate(held + held, axis=0).astype(jnp.float32).T
        for pair in range(2):
            stripes = [turn[pair, p * PACK : p * PACK + ORB] for p in range(WIDE)]
            stripes.append(turn[2, pair * narrow : (pair + 1) * narrow])
            flipped = jnp.concatenate(stripes, axis=0).astype(jnp.bfloat16)
            for a in range(2):
                atom = quad * 4 + pair * 2 + a
                for k in range(points):
                    dense = jnp.dot(
                        flipped, hot[atom, k], preferred_element_type=jnp.float32
                    ).astype(jnp.bfloat16)
                    for c in range(2):
                        base = pl.multiple_of((c * atoms + atom) * ORB, ORB)
                        for p in range(orbitals):
                            ham[k, pl.ds(base, ORB), p * LANES : (p + 1) * LANES] = dense[
                                p * ORB : (p + 1) * ORB, c * LANES : (c + 1) * LANES
                            ]
        return carry

    for c in range(CHUNKS):
        for other in others:
            block_copy(c, 0, other, other).wait_recv()
        lax.fori_loop(c * pairs // 2 // CHUNKS, (c + 1) * pairs // 2 // CHUNKS, build, 0)

    half = atoms * ORB

    outs = (first, second)

    def store(step, k):
        return pltpu.make_async_copy(made.at[step, k], outs[step].at[k], store_sem.at[step, k])

    def apply(step, k, window):
        prod[...] = jnp.dot(
            ham[k],
            window[k].reshape(orbitals * LANES, 2 * LANES),
            preferred_element_type=jnp.float32,
        )
        real = prod[0:half, 0:LANES] - prod[half : 2 * half, LANES : 2 * LANES]
        imag = prod[0:half, LANES : 2 * LANES] + prod[half : 2 * half, 0:LANES]
        for c, value in enumerate((real, imag)):
            for a in range(atoms):
                rows[pl.ds(a * pitch + c, orbitals, stride=2), :] = value[
                    a * ORB : a * ORB + orbitals
                ]
        made[step, k] = rows[0 : atoms * pitch, :].astype(jnp.bfloat16)
        store(step, k).start()

    for k in range(points):
        for copy in halo_copies(0, k, win, send_r):
            copy.wait_recv()
        apply(0, k, win)
        fill_window(k, win2, send_r2)
        for copy in halo_copies(1, k, win2, send_r2):
            copy.start()
    for k in range(points):
        for copy in halo_copies(1, k, win2, send_r2):
            copy.wait_recv()
        apply(1, k, win2)

    for c in range(CHUNKS):
        for d, other in enumerate(others):
            block_copy(c, d, z, other).wait_send()
    for k in range(points):
        for copy in halo_copies(0, k, win, send_r) + halo_copies(1, k, win2, send_r2):
            copy.wait_send()
        for step in range(2):
            store(step, k).wait()


def per_device(blocks, vectors, kvecs, neighbours, offsets, counts):
    n_atoms, n_kpt = lax.axis_size("atoms"), lax.axis_size("kpt")
    atoms, eight, orbitals, _ = blocks.shape
    slots = neighbours.shape[1]
    points = vectors.shape[0]
    flat_vectors = vectors.transpose(0, 1, 3, 2, 4).reshape(points, atoms * 2 * orbitals, LANES)
    depth = orbitals * LANES
    bf16, f32 = jnp.bfloat16, jnp.float32
    hbm = pl.BlockSpec(memory_space=pltpu.HBM)
    flops = 2 * points * 2 * 2 * atoms * ORB * depth * 2 * LANES
    args = (
        blocks.transpose(2, 3, 1, 0), flat_vectors, neighbours.T, offsets.T, counts[None, :],
        kvecs.T,
    )
    outs = pl.pallas_call(
        functools.partial(kernel, n_atoms, n_kpt),
        out_shape=[jax.ShapeDtypeStruct(flat_vectors.shape, bf16)] * 2,
        in_specs=[hbm] * len(args),
        out_specs=[hbm] * 2,
        scratch_shapes=[pltpu.VMEM(arg.shape, arg.dtype) for arg in args] + [
            pltpu.VMEM((n_kpt, atoms * eight * 3 // 2, LANES), bf16),
            pltpu.VMEM((points, 2 * atoms * ORB, depth), bf16),
            pltpu.VMEM((points, orbitals, LANES, 2 * LANES), bf16),
            pltpu.VMEM((points, orbitals, LANES, 2 * LANES), bf16),
            pltpu.VMEM((points, orbitals, REACH, 2 * LANES), bf16),
            pltpu.VMEM((points, orbitals, REACH, 2 * LANES), bf16),
            pltpu.VMEM((OWN * 2 * orbitals, LANES), f32),
            pltpu.VMEM((2 * atoms * ORB, 2 * LANES), f32),
            pltpu.VMEM((atoms, points, 4 * slots, 2 * LANES), bf16),
            pltpu.VMEM((atoms, 1 + 2 * points, slots, LANES), f32),
            pltpu.VMEM((LANES * 3 // 2 * eight, LANES), f32),
            pltpu.VMEM((2, atoms * eight, LANES), f32),
            pltpu.VMEM((3, LANES, LANES), f32),
            pltpu.VMEM((2,) + flat_vectors.shape, bf16),
            pltpu.SemaphoreType.DMA((CHUNKS, n_kpt - 1)),
            pltpu.SemaphoreType.DMA((CHUNKS, n_kpt)),
            pltpu.SemaphoreType.DMA((2, points, 2)),
            pltpu.SemaphoreType.DMA((2, points, 2)),
            pltpu.SemaphoreType.DMA((len(args),)),
            pltpu.SemaphoreType.DMA((2, points)),
        ],
        compiler_params=pltpu.CompilerParams(
            collective_id=0, has_side_effects=True, vmem_limit_bytes=60 * 1024 * 1024
        ),
        cost_estimate=pl.CostEstimate(flops=flops, bytes_accessed=4 << 20, transcendentals=0),
    )(*args)
    return tuple(
        out.reshape(points, atoms, orbitals, 2, LANES).transpose(0, 1, 3, 2, 4) for out in outs
    )


def solution(mesh):
    placed = (
        P("atoms", "kpt", None, None),
        P("kpt", "atoms", None, None, None),
        P(),
        P("atoms", None),
        P("atoms", None),
        P("atoms"),
    )
    return jax.shard_map(
        per_device,
        mesh=mesh,
        in_specs=placed,
        out_specs=(P("kpt", "atoms", None, None, None), P("kpt", "atoms", None, None, None)),
        check_vma=False,
    )
```

```python
import functools
import math

import jax
import jax.numpy as jnp
from jax import lax
from jax.experimental import pallas as pl
from jax.experimental.pallas import tpu as pltpu
from jax.sharding import PartitionSpec as P

REACH = 32
ORB = 16
LANES = 128
OWN = 48
LEFT = OWN
RIGHT = OWN + REACH
CHUNKS = 4
QUAD_ROWS = 48
HALF = 16
WIDE = 9
PACK = 14
MESH = pl.DeviceIdType.MESH


def kernel(
    n_atoms, n_kpt, blk_hbm, vec_hbm, near_hbm, shift_hbm, count_hbm, kvecs_hbm, first, second,
    blk, vec, near, shift, count, kvecs,
    gather, ham, win, win2, send_r, send_r2, rows, prod, hot, spread, tiles, flat, turn, made,
    blk_send, blk_recv, halo_send, halo_recv, load_sem, store_sem,
):
    loads = [
        pltpu.make_async_copy(source, held, load_sem.at[i])
        for i, (source, held) in enumerate(
            (
                (vec_hbm, vec), (blk_hbm, blk), (near_hbm, near),
                (shift_hbm, shift), (count_hbm, count), (kvecs_hbm, kvecs),
            )
        )
    ]
    for load in loads:
        load.start()
    points = vec.shape[0]
    orbitals, _, eight, atoms = blk.shape
    slots = near.shape[0]
    pairs = atoms // 2
    pitch = 2 * orbitals
    me = lax.axis_index("atoms")
    z = lax.axis_index("kpt")
    left, right = lax.rem(me + n_atoms - 1, n_atoms), lax.rem(me + 1, n_atoms)
    others = [lax.rem(z + d, n_kpt) for d in range(1, n_kpt)]

    barrier = pltpu.get_barrier_semaphore()
    for peer in (left, right):
        pl.semaphore_signal(barrier, inc=1, device_id=(peer, z), device_id_type=MESH)
    for other in others:
        pl.semaphore_signal(barrier, inc=1, device_id=(me, other), device_id_type=MESH)

    quads = atoms // 4
    split = (atoms - HALF) // 4
    cuts = [(0, split // 2), (split // 2, split), (split, (split + quads) // 2),
            ((split + quads) // 2, quads)]

    def block_copy(c, d, slab, other):
        part = pl.ds(cuts[c][0] * QUAD_ROWS, (cuts[c][1] - cuts[c][0]) * QUAD_ROWS)
        return pltpu.make_async_remote_copy(
            src_ref=gather.at[slab, part],
            dst_ref=gather.at[slab, part],
            send_sem=blk_send.at[c, d],
            recv_sem=blk_recv.at[c, slab],
            device_id=(me, other),
            device_id_type=MESH,
        )

    def halo_copies(step, k, window, to_right, part, start, size):
        return (
            pltpu.make_async_remote_copy(
                src_ref=to_right.at[k, :, pl.ds(start, size)],
                dst_ref=window.at[k, :, pl.ds(LEFT + start, size)],
                send_sem=halo_send.at[step, k, part, 0],
                recv_sem=halo_recv.at[step, k, part, 0],
                device_id=(right, z),
                device_id_type=MESH,
            ),
            pltpu.make_async_remote_copy(
                src_ref=window.at[k, :, pl.ds(start, size)],
                dst_ref=window.at[k, :, pl.ds(RIGHT + start, size)],
                send_sem=halo_send.at[step, k, part, 1],
                recv_sem=halo_recv.at[step, k, part, 1],
                device_id=(left, z),
                device_id_type=MESH,
            ),
        )

    def first_halo(k):
        return halo_copies(0, k, win, send_r, 0, 0, REACH)

    def second_halo(k, part):
        return halo_copies(1, k, win2, send_r2, part, part * HALF, HALF)

    def fill_window(k, window, to_right, own_rows, tail_rows):
        for p in range(orbitals):
            for c in range(2):
                lanes = pl.ds(c * LANES, LANES)
                (start, stop), at = own_rows, 2 * p + c
                own = rows[k, pl.ds(at + start * pitch, stop - start, stride=pitch), :]
                window[k, p, start:stop, lanes] = own.astype(jnp.bfloat16)
                start, stop = tail_rows
                at += (atoms - REACH + start) * pitch
                tail = rows[k, pl.ds(at, stop - start, stride=pitch), :]
                to_right[k, p, start:stop, lanes] = tail.astype(jnp.bfloat16)

    rows[:, atoms * pitch :, :] = jnp.zeros((points, (OWN - atoms) * pitch, LANES), jnp.float32)
    for p in range(WIDE):
        at = (p * PACK + orbitals) * eight
        tiles[at : at + eight, :] = jnp.zeros((eight, LANES), jnp.float32)
    tiles[WIDE * PACK * eight : LANES * eight, :] = jnp.zeros(
        ((LANES - WIDE * PACK) * eight, LANES), jnp.float32
    )
    for p in range(orbitals - WIDE):
        at = (LANES + p * ORB + orbitals) * eight
        tiles[at : at + (ORB - orbitals) * eight, :] = jnp.zeros(
            ((ORB - orbitals) * eight, LANES), jnp.float32
        )

    def send_vectors(k):
        rows[k, 0 : atoms * pitch, :] = vec[k].astype(jnp.float32)
        fill_window(k, win, send_r, (0, OWN), (0, REACH))
        if k == 0:
            pl.semaphore_wait(barrier, 2 + len(others))
        for copy in first_halo(k):
            copy.start()

    loads[0].wait()
    send_vectors(0)

    loads[1].wait()
    for p in range(orbitals):
        for o in range(orbitals):
            at = p * PACK + o if p < WIDE else LANES + (p - WIDE) * ORB + o
            tiles[at * eight : (at + 1) * eight, 0:atoms] = blk[o, p].astype(jnp.float32)
    narrow = LANES // 2
    for s in range(eight):
        wide = tiles[pl.ds(s, LANES, stride=eight), :]
        rest = tiles[pl.ds(LANES * eight + s, narrow, stride=eight), :]
        flat[0, pl.ds(s, atoms, stride=eight), :] = wide.T[:atoms]
        rest = jnp.concatenate([rest, rest], axis=0)
        flat[1, pl.ds(s, atoms, stride=eight), :] = rest.T[:atoms]
    even_side = lax.broadcasted_iota(jnp.int32, (16, LANES), 1) < narrow
    for quad in range(atoms // 4):
        at, to = quad * 32, quad * 48
        gather[z, to : to + 32] = flat[0, at : at + 32].astype(jnp.bfloat16)
        gather[z, to + 32 : to + 48] = jnp.where(
            even_side, flat[1, at : at + 16], flat[1, at + 16 : at + 32]
        ).astype(jnp.bfloat16)
    for c in range(CHUNKS):
        for d, other in enumerate(others):
            block_copy(c, d, z, other).start()
    for k in range(1, points):
        send_vectors(k)

    spare = pl.ds(RIGHT + REACH, LANES - RIGHT - REACH)
    for window in (win, win2):
        window[:, :, spare, :] = jnp.zeros(
            (points, orbitals, LANES - RIGHT - REACH, 2 * LANES), jnp.bfloat16
        )

    for load in loads[2:]:
        load.wait()
    total = atoms * n_atoms
    row = lax.broadcasted_iota(jnp.int32, (slots, atoms), 1)
    distance = near[...] - (me * atoms + row)
    distance = jnp.where(distance > total // 2, distance - total, distance)
    distance = jnp.where(distance < -(total // 2), distance + total, distance)
    local = row + distance
    place = jnp.where(
        local < 0, local + REACH + LEFT, jnp.where(local >= atoms, local - atoms + RIGHT, local)
    )
    live = lax.broadcasted_iota(jnp.int32, (slots, atoms), 0) < count[...]
    offset = shift[...].astype(jnp.float32)
    grid_row = jnp.floor((offset + 0.5) * (1.0 / 7.0))
    grid_col = offset - 7.0 * grid_row - 3.0
    grid_row = grid_row - 3.0
    columns = [place.astype(jnp.float32)]
    for k in range(points):
        own = lax.broadcasted_iota(jnp.int32, kvecs.shape, 1) == z * points + k
        kvec = jnp.sum(jnp.where(own, kvecs[...], 0.0), axis=1, keepdims=True)
        turns = kvec[0:1] * grid_row + kvec[1:2] * grid_col
        theta = (2.0 * math.pi) * (turns - jnp.floor(turns + 0.5))
        columns += [jnp.where(live, jnp.cos(theta), 0.0), jnp.where(live, jnp.sin(theta), 0.0)]
    for a in range(atoms):
        for j, column in enumerate(columns):
            spread[a, j] = jnp.broadcast_to(column[:, a : a + 1], (slots, LANES))

    lane = lax.broadcasted_iota(jnp.int32, (slots, LANES), 1).astype(jnp.float32)
    depth = 2 * slots
    nothing = jnp.zeros((eight, LANES), jnp.float32)

    def heat(pair, carry):
        for a in range(2):
            atom = 2 * pair + a
            hit = spread[atom, 0] == lane
            for k in range(points):
                for c in range(2):
                    value = jnp.where(hit, spread[atom, 1 + 2 * k + c], 0.0)
                    high = value.astype(jnp.bfloat16).astype(jnp.float32)
                    for part, piece in enumerate((high, value - high)):
                        laid = []
                        for s in range(n_kpt):
                            mine = piece[s * eight : (s + 1) * eight]
                            laid += [nothing, mine] if a else [mine, nothing]
                        hot[atom, k, part * depth : (part + 1) * depth,
                            c * LANES : (c + 1) * LANES] = jnp.concatenate(
                            laid, axis=0
                        ).astype(jnp.bfloat16)
        return carry

    lax.fori_loop(0, pairs, heat, 0)

    def build(quad, carry):
        at = pl.multiple_of(quad * 48, 16)
        for part in range(3):
            held = [gather[s, pl.ds(at + part * 16, 16), :] for s in range(n_kpt)]
            turn[part] = jnp.concatenate(held + held, axis=0).astype(jnp.float32).T
        for pair in range(2):
            stripes = [turn[pair, p * PACK : p * PACK + ORB] for p in range(WIDE)]
            stripes.append(turn[2, pair * narrow : (pair + 1) * narrow])
            flipped = jnp.concatenate(stripes, axis=0).astype(jnp.bfloat16)
            for a in range(2):
                atom = quad * 4 + pair * 2 + a
                for k in range(points):
                    dense = jnp.dot(
                        flipped, hot[atom, k], preferred_element_type=jnp.float32
                    ).astype(jnp.bfloat16)
                    for c in range(2):
                        base = pl.multiple_of(atom * ORB, ORB)
                        for p in range(orbitals):
                            ham[k, c, pl.ds(base, ORB), p * LANES : (p + 1) * LANES] = dense[
                                p * ORB : (p + 1) * ORB, c * LANES : (c + 1) * LANES
                            ]
        return carry

    outs = (first, second)

    def store(step, k):
        return pltpu.make_async_copy(made.at[step, k], outs[step].at[k], store_sem.at[step, k])

    def finish(step, k):
        made[step, k] = rows[k, 0 : atoms * pitch, :].astype(jnp.bfloat16)
        store(step, k).start()

    def apply(k, window, begin, end):
        count_rows = (end - begin) * ORB
        part = ham[k, :, begin * ORB : end * ORB].reshape(2 * count_rows, orbitals * LANES)
        prod[0 : 2 * count_rows] = jnp.dot(
            part,
            window[k].reshape(orbitals * LANES, 2 * LANES),
            preferred_element_type=jnp.float32,
        )
        low, high = slice(0, count_rows), slice(count_rows, 2 * count_rows)
        real = prod[low, 0:LANES] - prod[high, LANES : 2 * LANES]
        imag = prod[low, LANES : 2 * LANES] + prod[high, 0:LANES]
        for c, value in enumerate((real, imag)):
            for a in range(end - begin):
                rows[k, pl.ds((begin + a) * pitch + c, orbitals, stride=2), :] = value[
                    a * ORB : a * ORB + orbitals
                ]

    edges = (0, atoms - HALF, atoms)
    for part in range(2):
        for c in (2 * part, 2 * part + 1):
            for other in others:
                block_copy(c, 0, other, other).wait_recv()
            lax.fori_loop(cuts[c][0], cuts[c][1], build, 0)
        for k in range(points):
            if part == 0:
                for copy in first_halo(k):
                    copy.wait_recv()
            apply(k, win, edges[part], edges[part + 1])
            own_rows = ((0, HALF), (HALF, OWN))[part]
            fill_window(k, win2, send_r2, own_rows, (part * HALF, (part + 1) * HALF))
            for copy in second_halo(k, part):
                copy.start()
    for k in range(points):
        finish(0, k)
    for k in range(points):
        for part in range(2):
            for copy in second_halo(k, part):
                copy.wait_recv()
        apply(k, win2, 0, atoms)
        finish(1, k)

    for c in range(CHUNKS):
        for d, other in enumerate(others):
            block_copy(c, d, z, other).wait_send()
    for k in range(points):
        for copy in first_halo(k) + second_halo(k, 0) + second_halo(k, 1):
            copy.wait_send()
        for step in range(2):
            store(step, k).wait()


def hand_over(*refs):
    sems = refs[-1]
    arrays = len(refs) // 2
    copies = []
    for i in range(arrays):
        for k in range(refs[i].shape[0]):
            source, target = refs[i].at[k], refs[arrays + i].at[k]
            copies.append(pltpu.make_async_copy(source, target, sems.at[i, k]))
    for copy in copies:
        copy.start()
    for copy in copies:
        copy.wait()


def per_device(blocks, vectors, kvecs, neighbours, offsets, counts):
    n_atoms, n_kpt = lax.axis_size("atoms"), lax.axis_size("kpt")
    atoms, eight, orbitals, _ = blocks.shape
    slots = neighbours.shape[1]
    points = vectors.shape[0]
    flat_vectors = vectors.transpose(0, 1, 3, 2, 4).reshape(points, atoms * 2 * orbitals, LANES)
    depth = orbitals * LANES
    bf16, f32 = jnp.bfloat16, jnp.float32
    hbm = pl.BlockSpec(memory_space=pltpu.HBM)
    flops = 2 * points * 2 * 2 * atoms * ORB * depth * 2 * LANES
    args = (
        blocks.transpose(2, 3, 1, 0), flat_vectors, neighbours.T, offsets.T, counts[None, :],
        kvecs.T,
    )
    outs = pl.pallas_call(
        functools.partial(kernel, n_atoms, n_kpt),
        out_shape=[jax.ShapeDtypeStruct(flat_vectors.shape, bf16)] * 2,
        in_specs=[hbm] * len(args),
        out_specs=[hbm] * 2,
        scratch_shapes=[pltpu.VMEM(arg.shape, arg.dtype) for arg in args] + [
            pltpu.VMEM((n_kpt, atoms * eight * 3 // 2, LANES), bf16),
            pltpu.VMEM((points, 2, atoms * ORB, depth), bf16),
            pltpu.VMEM((points, orbitals, LANES, 2 * LANES), bf16),
            pltpu.VMEM((points, orbitals, LANES, 2 * LANES), bf16),
            pltpu.VMEM((points, orbitals, REACH, 2 * LANES), bf16),
            pltpu.VMEM((points, orbitals, REACH, 2 * LANES), bf16),
            pltpu.VMEM((points, OWN * 2 * orbitals, LANES), f32),
            pltpu.VMEM((2 * atoms * ORB, 2 * LANES), f32),
            pltpu.VMEM((atoms, points, 4 * slots, 2 * LANES), bf16),
            pltpu.VMEM((atoms, 1 + 2 * points, slots, LANES), f32),
            pltpu.VMEM((LANES * 3 // 2 * eight, LANES), f32),
            pltpu.VMEM((2, atoms * eight, LANES), f32),
            pltpu.VMEM((3, LANES, LANES), f32),
            pltpu.VMEM((2,) + flat_vectors.shape, bf16),
            pltpu.SemaphoreType.DMA((CHUNKS, n_kpt - 1)),
            pltpu.SemaphoreType.DMA((CHUNKS, n_kpt)),
            pltpu.SemaphoreType.DMA((2, points, 2, 2)),
            pltpu.SemaphoreType.DMA((2, points, 2, 2)),
            pltpu.SemaphoreType.DMA((len(args),)),
            pltpu.SemaphoreType.DMA((2, points)),
        ],
        compiler_params=pltpu.CompilerParams(
            collective_id=0, has_side_effects=True, vmem_limit_bytes=60 * 1024 * 1024
        ),
        cost_estimate=pl.CostEstimate(flops=flops, bytes_accessed=4 << 20, transcendentals=0),
    )(*args)
    outs = pl.pallas_call(
        hand_over,
        out_shape=[jax.ShapeDtypeStruct(flat_vectors.shape, bf16)] * 2,
        in_specs=[hbm] * 2,
        out_specs=[hbm] * 2,
        scratch_shapes=[pltpu.SemaphoreType.DMA((2, points))],
        compiler_params=pltpu.CompilerParams(vmem_limit_bytes=60 * 1024 * 1024),
        cost_estimate=pl.CostEstimate(flops=0, bytes_accessed=4 << 20, transcendentals=0),
    )(*outs)
    return tuple(
        out.reshape(points, atoms, orbitals, 2, LANES).transpose(0, 1, 3, 2, 4) for out in outs
    )


def solution(mesh):
    placed = (
        P("atoms", "kpt", None, None),
        P("kpt", "atoms", None, None, None),
        P(),
        P("atoms", None),
        P("atoms", None),
        P("atoms"),
    )
    return jax.shard_map(
        per_device,
        mesh=mesh,
        in_specs=placed,
        out_specs=(P("kpt", "atoms", None, None, None), P("kpt", "atoms", None, None, None)),
        check_vma=False,
    )
```

```python
import functools
import math

import jax
import jax.numpy as jnp
from jax import lax
from jax.experimental import pallas as pl
from jax.experimental.pallas import tpu as pltpu
from jax.sharding import PartitionSpec as P

REACH = 32
ORB = 16
LANES = 128
OWN = 48
LEFT = OWN
RIGHT = OWN + REACH
CHUNKS = 4
QUAD_ROWS = 48
HALF = 16
WIDE = 9
PACK = 14
MESH = pl.DeviceIdType.MESH


def kernel(
    n_atoms, n_kpt, blk_hbm, vec_hbm, near_hbm, shift_hbm, count_hbm, kvecs_hbm, first, second,
    blk, vec, near, shift, count, kvecs,
    gather, ham, win, win2, land, send_r2, rows, halo_rows, prod, hot, spread, tiles, flat, turn, made,
    blk_send, blk_recv, halo_send, halo_recv, load_sem, store_sem,
):
    loads = [
        pltpu.make_async_copy(source, held, load_sem.at[i])
        for i, (source, held) in enumerate(
            (
                (vec_hbm, vec), (blk_hbm, blk), (near_hbm, near),
                (shift_hbm, shift), (count_hbm, count), (kvecs_hbm, kvecs),
            )
        )
    ]
    for load in loads:
        load.start()
    points = made.shape[1]
    orbitals, _, eight, atoms = blk.shape
    slots = near.shape[0]
    pairs = atoms // 2
    pitch = 2 * orbitals
    me = lax.axis_index("atoms")
    z = lax.axis_index("kpt")
    left, right = lax.rem(me + n_atoms - 1, n_atoms), lax.rem(me + 1, n_atoms)
    others = [lax.rem(z + d, n_kpt) for d in range(1, n_kpt)]

    barrier = pltpu.get_barrier_semaphore()
    for peer in (left, right):
        pl.semaphore_signal(barrier, inc=1, device_id=(peer, z), device_id_type=MESH)
    for other in others:
        pl.semaphore_signal(barrier, inc=1, device_id=(me, other), device_id_type=MESH)

    quads = atoms // 4
    split = (atoms - HALF) // 4
    cuts = [(0, split // 2), (split // 2, split), (split, (split + quads) // 2),
            ((split + quads) // 2, quads)]

    def block_copy(c, d, slab, other):
        part = pl.ds(cuts[c][0] * QUAD_ROWS, (cuts[c][1] - cuts[c][0]) * QUAD_ROWS)
        return pltpu.make_async_remote_copy(
            src_ref=gather.at[slab, part],
            dst_ref=gather.at[slab, part],
            send_sem=blk_send.at[c, d],
            recv_sem=blk_recv.at[c, slab],
            device_id=(me, other),
            device_id_type=MESH,
        )

    def halo_copies(step, k, window, to_right, part, start, size):
        return (
            pltpu.make_async_remote_copy(
                src_ref=to_right.at[k, :, pl.ds(start, size)],
                dst_ref=window.at[k, :, pl.ds(LEFT + start, size)],
                send_sem=halo_send.at[step, k, part, 0],
                recv_sem=halo_recv.at[step, k, part, 0],
                device_id=(right, z),
                device_id_type=MESH,
            ),
            pltpu.make_async_remote_copy(
                src_ref=window.at[k, :, pl.ds(start, size)],
                dst_ref=window.at[k, :, pl.ds(RIGHT + start, size)],
                send_sem=halo_send.at[step, k, part, 1],
                recv_sem=halo_recv.at[step, k, part, 1],
                device_id=(left, z),
                device_id_type=MESH,
            ),
        )

    def raw_span(k, side):
        begin = (k * atoms + (0 if side else atoms - REACH)) * pitch
        start = begin // HALF * HALF
        stop = -(-(begin + REACH * pitch) // HALF) * HALF
        return start, stop - start, begin - start

    def first_halo(k):
        copies = []
        for side, peer in enumerate((right, left)):
            start, size, _ = raw_span(k, side)
            copies.append(
                pltpu.make_async_remote_copy(
                    src_ref=vec_hbm.at[pl.ds(start, size)],
                    dst_ref=land.at[k, side, pl.ds(0, size)],
                    send_sem=halo_send.at[0, k, 0, side],
                    recv_sem=halo_recv.at[0, k, 0, side],
                    device_id=(peer, z),
                    device_id_type=MESH,
                )
            )
        return tuple(copies)

    def lay_halo(k):
        for side, base in enumerate((LEFT, RIGHT)):
            _, size, skip = raw_span(k, side)
            halo_rows[side, 0:size] = land[k, side, 0:size].astype(jnp.float32)
            for p in range(orbitals):
                for c in range(2):
                    picked = halo_rows[side, pl.ds(skip + 2 * p + c, REACH, stride=pitch), :]
                    window_lanes = pl.ds(c * LANES, LANES)
                    win[k, p, base : base + REACH, window_lanes] = picked.astype(jnp.bfloat16)

    def second_halo(k, part):
        return halo_copies(1, k, win2, send_r2, part, part * HALF, HALF)

    def fill_window(k, window, to_right, own_rows, tail_rows):
        for p in range(orbitals):
            for c in range(2):
                lanes = pl.ds(c * LANES, LANES)
                (start, stop), at = own_rows, 2 * p + c
                own = rows[k, pl.ds(at + start * pitch, stop - start, stride=pitch), :]
                window[k, p, start:stop, lanes] = own.astype(jnp.bfloat16)
                if to_right is None:
                    continue
                start, stop = tail_rows
                at += (atoms - REACH + start) * pitch
                tail = rows[k, pl.ds(at, stop - start, stride=pitch), :]
                to_right[k, p, start:stop, lanes] = tail.astype(jnp.bfloat16)

    pl.semaphore_wait(barrier, 2 + len(others))
    for k in range(points):
        for copy in first_halo(k):
            copy.start()
    rows[:, atoms * pitch :, :] = jnp.zeros((points, (OWN - atoms) * pitch, LANES), jnp.float32)
    for p in range(WIDE):
        at = (p * PACK + orbitals) * eight
        tiles[at : at + eight, :] = jnp.zeros((eight, LANES), jnp.float32)
    tiles[WIDE * PACK * eight : LANES * eight, :] = jnp.zeros(
        ((LANES - WIDE * PACK) * eight, LANES), jnp.float32
    )
    for p in range(orbitals - WIDE):
        at = (LANES + p * ORB + orbitals) * eight
        tiles[at : at + (ORB - orbitals) * eight, :] = jnp.zeros(
            ((ORB - orbitals) * eight, LANES), jnp.float32
        )

    loads[1].wait()
    for p in range(orbitals):
        for o in range(orbitals):
            at = p * PACK + o if p < WIDE else LANES + (p - WIDE) * ORB + o
            tiles[at * eight : (at + 1) * eight, 0:atoms] = blk[o, p].astype(jnp.float32)
    narrow = LANES // 2
    for s in range(eight):
        wide = tiles[pl.ds(s, LANES, stride=eight), :]
        rest = tiles[pl.ds(LANES * eight + s, narrow, stride=eight), :]
        flat[0, pl.ds(s, atoms, stride=eight), :] = wide.T[:atoms]
        rest = jnp.concatenate([rest, rest], axis=0)
        flat[1, pl.ds(s, atoms, stride=eight), :] = rest.T[:atoms]
    even_side = lax.broadcasted_iota(jnp.int32, (16, LANES), 1) < narrow
    for quad in range(atoms // 4):
        at, to = quad * 32, quad * 48
        gather[z, to : to + 32] = flat[0, at : at + 32].astype(jnp.bfloat16)
        gather[z, to + 32 : to + 48] = jnp.where(
            even_side, flat[1, at : at + 16], flat[1, at + 16 : at + 32]
        ).astype(jnp.bfloat16)
    for c in range(CHUNKS):
        for d, other in enumerate(others):
            block_copy(c, d, z, other).start()
    loads[0].wait()
    for k in range(points):
        own_vectors = vec[k * atoms * pitch : (k + 1) * atoms * pitch]
        rows[k, 0 : atoms * pitch, :] = own_vectors.astype(jnp.float32)
        fill_window(k, win, None, (0, OWN), None)

    spare = pl.ds(RIGHT + REACH, LANES - RIGHT - REACH)
    for window in (win, win2):
        window[:, :, spare, :] = jnp.zeros(
            (points, orbitals, LANES - RIGHT - REACH, 2 * LANES), jnp.bfloat16
        )

    for load in loads[2:]:
        load.wait()
    total = atoms * n_atoms
    row = lax.broadcasted_iota(jnp.int32, (slots, atoms), 1)
    distance = near[...] - (me * atoms + row)
    distance = jnp.where(distance > total // 2, distance - total, distance)
    distance = jnp.where(distance < -(total // 2), distance + total, distance)
    local = row + distance
    place = jnp.where(
        local < 0, local + REACH + LEFT, jnp.where(local >= atoms, local - atoms + RIGHT, local)
    )
    live = lax.broadcasted_iota(jnp.int32, (slots, atoms), 0) < count[...]
    offset = shift[...].astype(jnp.float32)
    grid_row = jnp.floor((offset + 0.5) * (1.0 / 7.0))
    grid_col = offset - 7.0 * grid_row - 3.0
    grid_row = grid_row - 3.0
    columns = [place.astype(jnp.float32)]
    for k in range(points):
        own = lax.broadcasted_iota(jnp.int32, kvecs.shape, 1) == z * points + k
        kvec = jnp.sum(jnp.where(own, kvecs[...], 0.0), axis=1, keepdims=True)
        turns = kvec[0:1] * grid_row + kvec[1:2] * grid_col
        theta = (2.0 * math.pi) * (turns - jnp.floor(turns + 0.5))
        columns += [jnp.where(live, jnp.cos(theta), 0.0), jnp.where(live, jnp.sin(theta), 0.0)]
    for a in range(atoms):
        for j, column in enumerate(columns):
            spread[a, j] = jnp.broadcast_to(column[:, a : a + 1], (slots, LANES))

    lane = lax.broadcasted_iota(jnp.int32, (slots, LANES), 1).astype(jnp.float32)
    depth = 2 * slots
    nothing = jnp.zeros((eight, LANES), jnp.float32)

    def heat(pair, carry):
        for a in range(2):
            atom = 2 * pair + a
            hit = spread[atom, 0] == lane
            for k in range(points):
                for c in range(2):
                    value = jnp.where(hit, spread[atom, 1 + 2 * k + c], 0.0)
                    high = value.astype(jnp.bfloat16).astype(jnp.float32)
                    for part, piece in enumerate((high, value - high)):
                        laid = []
                        for s in range(n_kpt):
                            mine = piece[s * eight : (s + 1) * eight]
                            laid += [nothing, mine] if a else [mine, nothing]
                        hot[atom, k, part * depth : (part + 1) * depth,
                            c * LANES : (c + 1) * LANES] = jnp.concatenate(
                            laid, axis=0
                        ).astype(jnp.bfloat16)
        return carry

    lax.fori_loop(0, pairs, heat, 0, unroll=2)

    def build(quad, carry):
        at = pl.multiple_of(quad * 48, 16)
        for part in range(3):
            held = [gather[s, pl.ds(at + part * 16, 16), :] for s in range(n_kpt)]
            turn[part] = jnp.concatenate(held + held, axis=0).astype(jnp.float32).T
        for pair in range(2):
            stripes = [turn[pair, p * PACK : p * PACK + ORB] for p in range(WIDE)]
            stripes.append(turn[2, pair * narrow : (pair + 1) * narrow])
            flipped = jnp.concatenate(stripes, axis=0).astype(jnp.bfloat16)
            for a in range(2):
                atom = quad * 4 + pair * 2 + a
                for k in range(points):
                    dense = jnp.dot(
                        flipped, hot[atom, k], preferred_element_type=jnp.float32
                    ).astype(jnp.bfloat16)
                    for c in range(2):
                        base = pl.multiple_of(atom * ORB, ORB)
                        for p in range(orbitals):
                            ham[k, c, pl.ds(base, ORB), p * LANES : (p + 1) * LANES] = dense[
                                p * ORB : (p + 1) * ORB, c * LANES : (c + 1) * LANES
                            ]
        return carry

    outs = (first, second)

    def store(step, k):
        return pltpu.make_async_copy(made.at[step, k], outs[step].at[k], store_sem.at[step, k])

    def finish(step, k):
        made[step, k] = rows[k, 0 : atoms * pitch, :].astype(jnp.bfloat16)
        store(step, k).start()

    def apply(k, window, begin, end):
        count_rows = (end - begin) * ORB
        part = ham[k, :, begin * ORB : end * ORB].reshape(2 * count_rows, orbitals * LANES)
        prod[0 : 2 * count_rows] = jnp.dot(
            part,
            window[k].reshape(orbitals * LANES, 2 * LANES),
            preferred_element_type=jnp.float32,
        )
        low, high = slice(0, count_rows), slice(count_rows, 2 * count_rows)
        real = prod[low, 0:LANES] - prod[high, LANES : 2 * LANES]
        imag = prod[low, LANES : 2 * LANES] + prod[high, 0:LANES]
        for c, value in enumerate((real, imag)):
            for a in range(end - begin):
                rows[k, pl.ds((begin + a) * pitch + c, orbitals, stride=2), :] = value[
                    a * ORB : a * ORB + orbitals
                ]

    edges = (0, atoms - HALF, atoms)
    for part in range(2):
        for c in (2 * part, 2 * part + 1):
            for other in others:
                block_copy(c, 0, other, other).wait_recv()
            lax.fori_loop(cuts[c][0], cuts[c][1], build, 0, unroll=True)
        for k in range(points):
            if part == 0:
                for copy in first_halo(k):
                    copy.wait_recv()
                lay_halo(k)
            apply(k, win, edges[part], edges[part + 1])
            own_rows = ((0, HALF), (HALF, OWN))[part]
            fill_window(k, win2, send_r2, own_rows, (part * HALF, (part + 1) * HALF))
            for copy in second_halo(k, part):
                copy.start()
    for k in range(points):
        finish(0, k)
    for k in range(points):
        for part in range(2):
            for copy in second_halo(k, part):
                copy.wait_recv()
        apply(k, win2, 0, atoms)
        finish(1, k)

    for c in range(CHUNKS):
        for d, other in enumerate(others):
            block_copy(c, d, z, other).wait_send()
    for k in range(points):
        for copy in first_halo(k) + second_halo(k, 0) + second_halo(k, 1):
            copy.wait_send()
        for step in range(2):
            store(step, k).wait()


def hand_over(*refs):
    arrays = (len(refs) - 2) // 2
    held, sems = refs[-2], refs[-1]
    steps = []
    for i in range(arrays):
        for k in range(refs[i].shape[0]):
            source, target = refs[i].at[k], refs[arrays + i].at[k]
            here = held.at[i, k]
            steps.append((
                pltpu.make_async_copy(source, here, sems.at[0, i, k]),
                pltpu.make_async_copy(here, target, sems.at[1, i, k]),
            ))
    for fetch, _ in steps:
        fetch.start()
    for fetch, put in steps:
        fetch.wait()
        put.start()
    for _, put in steps:
        put.wait()


def per_device(blocks, vectors, kvecs, neighbours, offsets, counts):
    n_atoms, n_kpt = lax.axis_size("atoms"), lax.axis_size("kpt")
    atoms, eight, orbitals, _ = blocks.shape
    slots = neighbours.shape[1]
    points = vectors.shape[0]
    per_point = (points, atoms * 2 * orbitals, LANES)
    flat_vectors = vectors.transpose(0, 1, 3, 2, 4).reshape(points * per_point[1], LANES)
    landing = -(-(REACH * 2 * orbitals) // HALF) * HALF + HALF
    depth = orbitals * LANES
    bf16, f32 = jnp.bfloat16, jnp.float32
    hbm = pl.BlockSpec(memory_space=pltpu.HBM)
    flops = 2 * points * 2 * 2 * atoms * ORB * depth * 2 * LANES
    args = (
        blocks.transpose(2, 3, 1, 0), flat_vectors, neighbours.T, offsets.T, counts[None, :],
        kvecs.T,
    )
    outs = pl.pallas_call(
        functools.partial(kernel, n_atoms, n_kpt),
        out_shape=[jax.ShapeDtypeStruct(per_point, bf16)] * 2,
        in_specs=[hbm] * len(args),
        out_specs=[hbm] * 2,
        scratch_shapes=[pltpu.VMEM(arg.shape, arg.dtype) for arg in args] + [
            pltpu.VMEM((n_kpt, atoms * eight * 3 // 2, LANES), bf16),
            pltpu.VMEM((points, 2, atoms * ORB, depth), bf16),
            pltpu.VMEM((points, orbitals, LANES, 2 * LANES), bf16),
            pltpu.VMEM((points, orbitals, LANES, 2 * LANES), bf16),
            pltpu.VMEM((points, 2, landing, LANES), bf16),
            pltpu.VMEM((points, orbitals, REACH, 2 * LANES), bf16),
            pltpu.VMEM((points, OWN * 2 * orbitals, LANES), f32),
            pltpu.VMEM((2, landing, LANES), f32),
            pltpu.VMEM((2 * atoms * ORB, 2 * LANES), f32),
            pltpu.VMEM((atoms, points, 4 * slots, 2 * LANES), bf16),
            pltpu.VMEM((atoms, 1 + 2 * points, slots, LANES), f32),
            pltpu.VMEM((LANES * 3 // 2 * eight, LANES), f32),
            pltpu.VMEM((2, atoms * eight, LANES), f32),
            pltpu.VMEM((3, LANES, LANES), f32),
            pltpu.VMEM((2,) + per_point, bf16),
            pltpu.SemaphoreType.DMA((CHUNKS, n_kpt - 1)),
            pltpu.SemaphoreType.DMA((CHUNKS, n_kpt)),
            pltpu.SemaphoreType.DMA((2, points, 2, 2)),
            pltpu.SemaphoreType.DMA((2, points, 2, 2)),
            pltpu.SemaphoreType.DMA((len(args),)),
            pltpu.SemaphoreType.DMA((2, points)),
        ],
        compiler_params=pltpu.CompilerParams(
            collective_id=0, has_side_effects=True, vmem_limit_bytes=60 * 1024 * 1024
        ),
        cost_estimate=pl.CostEstimate(flops=flops, bytes_accessed=4 << 20, transcendentals=0),
    )(*args)
    outs = pl.pallas_call(
        hand_over,
        out_shape=[jax.ShapeDtypeStruct(per_point, bf16)] * 2,
        in_specs=[hbm] * 2,
        out_specs=[hbm] * 2,
        scratch_shapes=[
            pltpu.VMEM((2,) + per_point, bf16),
            pltpu.SemaphoreType.DMA((2, 2, points)),
        ],
        compiler_params=pltpu.CompilerParams(vmem_limit_bytes=60 * 1024 * 1024),
        cost_estimate=pl.CostEstimate(flops=0, bytes_accessed=4 << 20, transcendentals=0),
    )(*outs)
    return tuple(
        out.reshape(points, atoms, orbitals, 2, LANES).transpose(0, 1, 3, 2, 4) for out in outs
    )


def solution(mesh):
    placed = (
        P("atoms", "kpt", None, None),
        P("kpt", "atoms", None, None, None),
        P(),
        P("atoms", None),
        P("atoms", None),
        P("atoms"),
    )
    return jax.shard_map(
        per_device,
        mesh=mesh,
        in_specs=placed,
        out_specs=(P("kpt", "atoms", None, None, None), P("kpt", "atoms", None, None, None)),
        check_vma=False,
    )
```

```python
import functools
import math

import jax
import jax.numpy as jnp
from jax import lax
from jax.experimental import pallas as pl
from jax.experimental.pallas import tpu as pltpu
from jax.sharding import PartitionSpec as P

REACH = 32
ORB = 16
LANES = 128
OWN = 48
LEFT = OWN
RIGHT = OWN + REACH
CHUNKS = 4
QUAD_ROWS = 48
HALF = 16
WIDE = 9
PACK = 14
MESH = pl.DeviceIdType.MESH


def kernel(
    n_atoms, n_kpt, blk_hbm, vec_hbm, near_hbm, shift_hbm, count_hbm, kvecs_hbm, first, second,
    blk, vec, near, shift, count, kvecs,
    gather, ham, win, win2, land, send_r2, rows, halo_rows, prod, hot, spread, tiles, flat, turn,
    blk_send, blk_recv, halo_send, halo_recv, load_sem,
):
    loads = [
        pltpu.make_async_copy(source, held, load_sem.at[i])
        for i, (source, held) in enumerate(
            (
                (vec_hbm, vec), (blk_hbm, blk), (near_hbm, near),
                (shift_hbm, shift), (count_hbm, count), (kvecs_hbm, kvecs),
            )
        )
    ]
    for load in loads:
        load.start()
    points = first.shape[0]
    orbitals, _, eight, atoms = blk.shape
    slots = near.shape[0]
    pairs = atoms // 2
    pitch = 2 * orbitals
    me = lax.axis_index("atoms")
    z = lax.axis_index("kpt")
    left, right = lax.rem(me + n_atoms - 1, n_atoms), lax.rem(me + 1, n_atoms)
    others = [lax.rem(z + d, n_kpt) for d in range(1, n_kpt)]

    barrier = pltpu.get_barrier_semaphore()
    for peer in (left, right):
        pl.semaphore_signal(barrier, inc=1, device_id=(peer, z), device_id_type=MESH)
    for other in others:
        pl.semaphore_signal(barrier, inc=1, device_id=(me, other), device_id_type=MESH)

    quads = atoms // 4
    split = (atoms - HALF) // 4
    cuts = [(0, split // 2), (split // 2, split), (split, (split + quads) // 2),
            ((split + quads) // 2, quads)]

    def hop(c, way, slab):
        part = pl.ds(cuts[c][0] * QUAD_ROWS, (cuts[c][1] - cuts[c][0]) * QUAD_ROWS)
        return pltpu.make_async_remote_copy(
            src_ref=gather.at[slab, part],
            dst_ref=gather.at[slab, part],
            send_sem=blk_send.at[c, way, slab],
            recv_sem=blk_recv.at[c, slab],
            device_id=(me, z + 1 if way else z - 1),
            device_id_type=MESH,
        )

    def outgoing(c, step, act):
        @pl.when(jnp.logical_and(z - step >= 0, z + 1 < n_kpt))
        def _():
            if act == "pass" and step:
                hop(c, 1, z - step).wait_recv()
            if act == "pass":
                hop(c, 1, z - step).start()
            else:
                hop(c, 1, z - step).wait_send()

        @pl.when(jnp.logical_and(z + step < n_kpt, z - 1 >= 0))
        def _():
            if act == "pass" and step:
                hop(c, 0, z + step).wait_recv()
            if act == "pass":
                hop(c, 0, z + step).start()
            else:
                hop(c, 0, z + step).wait_send()

    def final_arrivals(c):
        @pl.when(z + 1 == n_kpt)
        def _():
            for slab in range(n_kpt - 1):
                hop(c, 0, slab).wait_recv()

        @pl.when(z == 0)
        def _():
            for slab in range(1, n_kpt):
                hop(c, 1, slab).wait_recv()

    def halo_copies(step, k, window, to_right, part, start, size):
        return (
            pltpu.make_async_remote_copy(
                src_ref=to_right.at[k, :, pl.ds(start, size)],
                dst_ref=window.at[k, :, pl.ds(LEFT + start, size)],
                send_sem=halo_send.at[step, k, part, 0],
                recv_sem=halo_recv.at[step, k, part, 0],
                device_id=(right, z),
                device_id_type=MESH,
            ),
            pltpu.make_async_remote_copy(
                src_ref=window.at[k, :, pl.ds(start, size)],
                dst_ref=window.at[k, :, pl.ds(RIGHT + start, size)],
                send_sem=halo_send.at[step, k, part, 1],
                recv_sem=halo_recv.at[step, k, part, 1],
                device_id=(left, z),
                device_id_type=MESH,
            ),
        )

    def raw_span(k, side):
        begin = (k * atoms + (0 if side else atoms - REACH)) * pitch
        start = begin // HALF * HALF
        stop = -(-(begin + REACH * pitch) // HALF) * HALF
        return start, stop - start, begin - start

    def first_halo(k):
        copies = []
        for side, peer in enumerate((right, left)):
            start, size, _ = raw_span(k, side)
            copies.append(
                pltpu.make_async_remote_copy(
                    src_ref=vec_hbm.at[pl.ds(start, size)],
                    dst_ref=land.at[k, side, pl.ds(0, size)],
                    send_sem=halo_send.at[0, k, 0, side],
                    recv_sem=halo_recv.at[0, k, 0, side],
                    device_id=(peer, z),
                    device_id_type=MESH,
                )
            )
        return tuple(copies)

    def lay_halo(k):
        for side, base in enumerate((LEFT, RIGHT)):
            _, size, skip = raw_span(k, side)
            halo_rows[side, 0:size] = land[k, side, 0:size].astype(jnp.float32)
            for p in range(orbitals):
                for c in range(2):
                    picked = halo_rows[side, pl.ds(skip + 2 * p + c, REACH, stride=pitch), :]
                    window_lanes = pl.ds(c * LANES, LANES)
                    win[k, p, base : base + REACH, window_lanes] = picked.astype(jnp.bfloat16)

    def second_halo(k, part):
        return halo_copies(1, k, win2, send_r2, part, part * HALF, HALF)

    def fill_window(k, window, to_right, own_rows, tail_rows):
        for p in range(orbitals):
            for c in range(2):
                lanes = pl.ds(c * LANES, LANES)
                (start, stop), at = own_rows, 2 * p + c
                own = rows[k, pl.ds(at + start * pitch, stop - start, stride=pitch), :]
                window[k, p, start:stop, lanes] = own.astype(jnp.bfloat16)
                if to_right is None:
                    continue
                start, stop = tail_rows
                at += (atoms - REACH + start) * pitch
                tail = rows[k, pl.ds(at, stop - start, stride=pitch), :]
                to_right[k, p, start:stop, lanes] = tail.astype(jnp.bfloat16)

    pl.semaphore_wait(barrier, 2 + len(others))
    for k in range(points):
        for copy in first_halo(k):
            copy.start()
    rows[:, atoms * pitch :, :] = jnp.zeros((points, (OWN - atoms) * pitch, LANES), jnp.float32)
    for p in range(WIDE):
        at = (p * PACK + orbitals) * eight
        tiles[at : at + eight, :] = jnp.zeros((eight, LANES), jnp.float32)
    tiles[WIDE * PACK * eight : LANES * eight, :] = jnp.zeros(
        ((LANES - WIDE * PACK) * eight, LANES), jnp.float32
    )
    for p in range(orbitals - WIDE):
        at = (LANES + p * ORB + orbitals) * eight
        tiles[at : at + (ORB - orbitals) * eight, :] = jnp.zeros(
            ((ORB - orbitals) * eight, LANES), jnp.float32
        )

    loads[1].wait()
    for p in range(orbitals):
        for o in range(orbitals):
            at = p * PACK + o if p < WIDE else LANES + (p - WIDE) * ORB + o
            tiles[at * eight : (at + 1) * eight, 0:atoms] = blk[o, p].astype(jnp.float32)
    narrow = LANES // 2
    for s in range(eight):
        wide = tiles[pl.ds(s, LANES, stride=eight), :]
        rest = tiles[pl.ds(LANES * eight + s, narrow, stride=eight), :]
        flat[0, pl.ds(s, atoms, stride=eight), :] = wide.T[:atoms]
        rest = jnp.concatenate([rest, rest], axis=0)
        flat[1, pl.ds(s, atoms, stride=eight), :] = rest.T[:atoms]
    even_side = lax.broadcasted_iota(jnp.int32, (16, LANES), 1) < narrow
    for quad in range(atoms // 4):
        at, to = quad * 32, quad * 48
        gather[z, to : to + 32] = flat[0, at : at + 32].astype(jnp.bfloat16)
        gather[z, to + 32 : to + 48] = jnp.where(
            even_side, flat[1, at : at + 16], flat[1, at + 16 : at + 32]
        ).astype(jnp.bfloat16)
    for c in range(CHUNKS):
        outgoing(c, 0, "pass")
    loads[0].wait()
    for k in range(points):
        own_vectors = vec[k * atoms * pitch : (k + 1) * atoms * pitch]
        rows[k, 0 : atoms * pitch, :] = own_vectors.astype(jnp.float32)
        fill_window(k, win, None, (0, OWN), None)

    spare = pl.ds(RIGHT + REACH, LANES - RIGHT - REACH)
    for window in (win, win2):
        window[:, :, spare, :] = jnp.zeros(
            (points, orbitals, LANES - RIGHT - REACH, 2 * LANES), jnp.bfloat16
        )

    for load in loads[2:]:
        load.wait()
    total = atoms * n_atoms
    row = lax.broadcasted_iota(jnp.int32, (slots, atoms), 1)
    distance = near[...] - (me * atoms + row)
    distance = jnp.where(distance > total // 2, distance - total, distance)
    distance = jnp.where(distance < -(total // 2), distance + total, distance)
    local = row + distance
    place = jnp.where(
        local < 0, local + REACH + LEFT, jnp.where(local >= atoms, local - atoms + RIGHT, local)
    )
    live = lax.broadcasted_iota(jnp.int32, (slots, atoms), 0) < count[...]
    offset = shift[...].astype(jnp.float32)
    grid_row = jnp.floor((offset + 0.5) * (1.0 / 7.0))
    grid_col = offset - 7.0 * grid_row - 3.0
    grid_row = grid_row - 3.0
    columns = [place.astype(jnp.float32)]
    for k in range(points):
        own = lax.broadcasted_iota(jnp.int32, kvecs.shape, 1) == z * points + k
        kvec = jnp.sum(jnp.where(own, kvecs[...], 0.0), axis=1, keepdims=True)
        turns = kvec[0:1] * grid_row + kvec[1:2] * grid_col
        theta = (2.0 * math.pi) * (turns - jnp.floor(turns + 0.5))
        columns += [jnp.where(live, jnp.cos(theta), 0.0), jnp.where(live, jnp.sin(theta), 0.0)]
    outgoing(0, 1, "pass")
    outgoing(1, 1, "pass")
    for a in range(atoms):
        for j, column in enumerate(columns):
            spread[a, j] = jnp.broadcast_to(column[:, a : a + 1], (slots, LANES))

    lane = lax.broadcasted_iota(jnp.int32, (slots, LANES), 1).astype(jnp.float32)
    depth = 2 * slots
    nothing = jnp.zeros((eight, LANES), jnp.float32)

    def heat(pair, carry):
        for a in range(2):
            atom = 2 * pair + a
            hit = spread[atom, 0] == lane
            for k in range(points):
                for c in range(2):
                    value = jnp.where(hit, spread[atom, 1 + 2 * k + c], 0.0)
                    high = value.astype(jnp.bfloat16).astype(jnp.float32)
                    for part, piece in enumerate((high, value - high)):
                        laid = []
                        for s in range(n_kpt):
                            mine = piece[s * eight : (s + 1) * eight]
                            laid += [nothing, mine] if a else [mine, nothing]
                        hot[atom, k, part * depth : (part + 1) * depth,
                            c * LANES : (c + 1) * LANES] = jnp.concatenate(
                            laid, axis=0
                        ).astype(jnp.bfloat16)
        return carry

    lax.fori_loop(0, pairs // 2, heat, 0, unroll=2)
    outgoing(2, 1, "pass")
    outgoing(3, 1, "pass")
    for c in range(2):
        outgoing(c, 2, "pass")
    lax.fori_loop(pairs // 2, pairs, heat, 0, unroll=2)

    def build(quad, carry):
        at = pl.multiple_of(quad * 48, 16)
        for part in range(3):
            held = [gather[s, pl.ds(at + part * 16, 16), :] for s in range(n_kpt)]
            turn[part] = jnp.concatenate(held + held, axis=0).astype(jnp.float32).T
        for pair in range(2):
            stripes = [turn[pair, p * PACK : p * PACK + ORB] for p in range(WIDE)]
            stripes.append(turn[2, pair * narrow : (pair + 1) * narrow])
            flipped = jnp.concatenate(stripes, axis=0).astype(jnp.bfloat16)
            for a in range(2):
                atom = quad * 4 + pair * 2 + a
                for k in range(points):
                    dense = jnp.dot(
                        flipped, hot[atom, k], preferred_element_type=jnp.float32
                    ).astype(jnp.bfloat16)
                    for c in range(2):
                        base = pl.multiple_of(atom * ORB, ORB)
                        for p in range(orbitals):
                            ham[k, c, pl.ds(base, ORB), p * LANES : (p + 1) * LANES] = dense[
                                p * ORB : (p + 1) * ORB, c * LANES : (c + 1) * LANES
                            ]
        return carry

    outs = (first, second)

    def finish(step, k):
        outs[step][k] = rows[k, 0 : atoms * pitch, :].astype(jnp.bfloat16)

    def apply(k, window, begin, end):
        count_rows = (end - begin) * ORB
        part = ham[k, :, begin * ORB : end * ORB].reshape(2 * count_rows, orbitals * LANES)
        prod[0 : 2 * count_rows] = jnp.dot(
            part,
            window[k].reshape(orbitals * LANES, 2 * LANES),
            preferred_element_type=jnp.float32,
        )
        low, high = slice(0, count_rows), slice(count_rows, 2 * count_rows)
        real = prod[low, 0:LANES] - prod[high, LANES : 2 * LANES]
        imag = prod[low, LANES : 2 * LANES] + prod[high, 0:LANES]
        for c, value in enumerate((real, imag)):
            for a in range(end - begin):
                rows[k, pl.ds((begin + a) * pitch + c, orbitals, stride=2), :] = value[
                    a * ORB : a * ORB + orbitals
                ]

    edges = (0, atoms - HALF, atoms)
    for part in range(2):
        for c in (2 * part, 2 * part + 1):
            final_arrivals(c)
            lax.fori_loop(cuts[c][0], cuts[c][1], build, 0, unroll=True)
            if part == 0:
                outgoing(c + 2, 2, "pass")
        for k in range(points):
            if part == 0:
                for copy in first_halo(k):
                    copy.wait_recv()
                lay_halo(k)
            apply(k, win, edges[part], edges[part + 1])
            own_rows = ((0, HALF), (HALF, OWN))[part]
            fill_window(k, win2, send_r2, own_rows, (part * HALF, (part + 1) * HALF))
            for copy in second_halo(k, part):
                copy.start()
    for k in range(points):
        finish(0, k)
    for k in range(points):
        for part in range(2):
            for copy in second_halo(k, part):
                copy.wait_recv()
        apply(k, win2, 0, atoms)
        finish(1, k)

    for c in range(CHUNKS):
        for step in range(n_kpt - 1):
            outgoing(c, step, "done")
    for k in range(points):
        for copy in first_halo(k) + second_halo(k, 0) + second_halo(k, 1):
            copy.wait_send()


def hand_over(*refs):
    arrays = len(refs) // 2
    sems = refs[-1]
    copies = []
    for i in range(arrays):
        for k in range(refs[i].shape[0]):
            copies.append(
                pltpu.make_async_copy(refs[i].at[k], refs[arrays + i].at[k], sems.at[i, k])
            )
    for copy in copies:
        copy.start()
    for copy in copies:
        copy.wait()


def per_device(blocks, vectors, kvecs, neighbours, offsets, counts):
    n_atoms, n_kpt = lax.axis_size("atoms"), lax.axis_size("kpt")
    atoms, eight, orbitals, _ = blocks.shape
    slots = neighbours.shape[1]
    points = vectors.shape[0]
    per_point = (points, atoms * 2 * orbitals, LANES)
    flat_vectors = vectors.transpose(0, 1, 3, 2, 4).reshape(points * per_point[1], LANES)
    landing = -(-(REACH * 2 * orbitals) // HALF) * HALF + HALF
    depth = orbitals * LANES
    bf16, f32 = jnp.bfloat16, jnp.float32
    hbm = pl.BlockSpec(memory_space=pltpu.HBM)
    vmem = pl.BlockSpec(memory_space=pltpu.VMEM)
    flops = 2 * points * 2 * 2 * atoms * ORB * depth * 2 * LANES
    args = (
        blocks.transpose(2, 3, 1, 0), flat_vectors, neighbours.T, offsets.T, counts[None, :],
        kvecs.T,
    )
    outs = pl.pallas_call(
        functools.partial(kernel, n_atoms, n_kpt),
        out_shape=[jax.ShapeDtypeStruct(per_point, bf16)] * 2,
        in_specs=[hbm] * len(args),
        out_specs=[vmem] * 2,
        scratch_shapes=[pltpu.VMEM(arg.shape, arg.dtype) for arg in args] + [
            pltpu.VMEM((n_kpt, atoms * eight * 3 // 2, LANES), bf16),
            pltpu.VMEM((points, 2, atoms * ORB, depth), bf16),
            pltpu.VMEM((points, orbitals, LANES, 2 * LANES), bf16),
            pltpu.VMEM((points, orbitals, LANES, 2 * LANES), bf16),
            pltpu.VMEM((points, 2, landing, LANES), bf16),
            pltpu.VMEM((points, orbitals, REACH, 2 * LANES), bf16),
            pltpu.VMEM((points, OWN * 2 * orbitals, LANES), f32),
            pltpu.VMEM((2, landing, LANES), f32),
            pltpu.VMEM((2 * atoms * ORB, 2 * LANES), f32),
            pltpu.VMEM((atoms, points, 4 * slots, 2 * LANES), bf16),
            pltpu.VMEM((atoms, 1 + 2 * points, slots, LANES), f32),
            pltpu.VMEM((LANES * 3 // 2 * eight, LANES), f32),
            pltpu.VMEM((2, atoms * eight, LANES), f32),
            pltpu.VMEM((3, LANES, LANES), f32),
            pltpu.SemaphoreType.DMA((CHUNKS, 2, n_kpt)),
            pltpu.SemaphoreType.DMA((CHUNKS, n_kpt)),
            pltpu.SemaphoreType.DMA((2, points, 2, 2)),
            pltpu.SemaphoreType.DMA((2, points, 2, 2)),
            pltpu.SemaphoreType.DMA((len(args),)),
        ],
        compiler_params=pltpu.CompilerParams(
            collective_id=0, has_side_effects=True, vmem_limit_bytes=60 * 1024 * 1024
        ),
        cost_estimate=pl.CostEstimate(flops=flops, bytes_accessed=4 << 20, transcendentals=0),
    )(*args)
    outs = pl.pallas_call(
        hand_over,
        out_shape=[jax.ShapeDtypeStruct(per_point, bf16)] * 2,
        in_specs=[vmem] * 2,
        out_specs=[hbm] * 2,
        scratch_shapes=[pltpu.SemaphoreType.DMA((2, points))],
        compiler_params=pltpu.CompilerParams(vmem_limit_bytes=4 * 1024 * 1024),
        cost_estimate=pl.CostEstimate(flops=0, bytes_accessed=4 << 20, transcendentals=0),
    )(*outs)
    return tuple(
        out.reshape(points, atoms, orbitals, 2, LANES).transpose(0, 1, 3, 2, 4) for out in outs
    )


def solution(mesh):
    placed = (
        P("atoms", "kpt", None, None),
        P("kpt", "atoms", None, None, None),
        P(),
        P("atoms", None),
        P("atoms", None),
        P("atoms"),
    )
    return jax.shard_map(
        per_device,
        mesh=mesh,
        in_specs=placed,
        out_specs=(P("kpt", "atoms", None, None, None), P("kpt", "atoms", None, None, None)),
        check_vma=False,
    )
```

```python
import functools
import math

import jax
import jax.numpy as jnp
from jax import lax
from jax.experimental import pallas as pl
from jax.experimental.pallas import tpu as pltpu
from jax.sharding import PartitionSpec as P

REACH = 32
ORB = 16
LANES = 128
OWN = 48
LEFT = OWN
RIGHT = OWN + REACH
CHUNKS = 4
PIECES = 8
QUAD_ROWS = 48
HALF = 16
WIDE = 9
PACK = 14
MESH = pl.DeviceIdType.MESH


def kernel(
    n_atoms, n_kpt, blk_hbm, vec_hbm, near_hbm, shift_hbm, count_hbm, kvecs_hbm, first, second,
    blk, vec, near, shift, count, kvecs,
    gather, ham, win, win2, land, send_r2, rows, halo_rows, prod, hot, spread, tiles, flat, turn, made,
    blk_send, blk_recv, halo_send, halo_recv, load_sem, store_sem,
):
    loads = [
        pltpu.make_async_copy(source, held, load_sem.at[i])
        for i, (source, held) in enumerate(
            (
                (vec_hbm, vec), (blk_hbm, blk), (near_hbm, near),
                (shift_hbm, shift), (count_hbm, count), (kvecs_hbm, kvecs),
            )
        )
    ]
    for load in loads:
        load.start()
    points = made.shape[1]
    orbitals, _, eight, atoms = blk.shape
    slots = near.shape[0]
    pairs = atoms // 2
    pitch = 2 * orbitals
    me = lax.axis_index("atoms")
    z = lax.axis_index("kpt")
    left, right = lax.rem(me + n_atoms - 1, n_atoms), lax.rem(me + 1, n_atoms)
    others = [lax.rem(z + d, n_kpt) for d in range(1, n_kpt)]

    barrier = pltpu.get_barrier_semaphore()
    for peer in (left, right):
        pl.semaphore_signal(barrier, inc=1, device_id=(peer, z), device_id_type=MESH)
    for other in others:
        pl.semaphore_signal(barrier, inc=1, device_id=(me, other), device_id_type=MESH)

    quads = atoms // 4
    split = (atoms - HALF) // 4
    cuts = [(0, split // 2), (split // 2, split), (split, (split + quads) // 2),
            ((split + quads) // 2, quads)]

    def block_copy(c, d, slab, other):
        part = pl.ds(cuts[c][0] * QUAD_ROWS, (cuts[c][1] - cuts[c][0]) * QUAD_ROWS)
        return pltpu.make_async_remote_copy(
            src_ref=gather.at[slab, part],
            dst_ref=gather.at[slab, part],
            send_sem=blk_send.at[c, d],
            recv_sem=blk_recv.at[c, slab],
            device_id=(me, other),
            device_id_type=MESH,
        )

    def halo_copies(step, k, window, to_right, part, start, size):
        return (
            pltpu.make_async_remote_copy(
                src_ref=to_right.at[k, :, pl.ds(start, size)],
                dst_ref=window.at[k, :, pl.ds(LEFT + start, size)],
                send_sem=halo_send.at[step, k, part, 0],
                recv_sem=halo_recv.at[step, k, part, 0],
                device_id=(right, z),
                device_id_type=MESH,
            ),
            pltpu.make_async_remote_copy(
                src_ref=window.at[k, :, pl.ds(start, size)],
                dst_ref=window.at[k, :, pl.ds(RIGHT + start, size)],
                send_sem=halo_send.at[step, k, part, 1],
                recv_sem=halo_recv.at[step, k, part, 1],
                device_id=(left, z),
                device_id_type=MESH,
            ),
        )

    def raw_span(k, side):
        begin = (k * atoms + (0 if side else atoms - REACH)) * pitch
        start = begin // HALF * HALF
        stop = -(-(begin + REACH * pitch) // HALF) * HALF
        return start, stop - start, begin - start

    def first_halo(k):
        copies = []
        for side, peer in enumerate((right, left)):
            start, size, _ = raw_span(k, side)
            copies.append(
                pltpu.make_async_remote_copy(
                    src_ref=vec_hbm.at[pl.ds(start, size)],
                    dst_ref=land.at[k, side, pl.ds(0, size)],
                    send_sem=halo_send.at[0, k, 0, side],
                    recv_sem=halo_recv.at[0, k, 0, side],
                    device_id=(peer, z),
                    device_id_type=MESH,
                )
            )
        return tuple(copies)

    def lay_halo(k):
        for side, base in enumerate((LEFT, RIGHT)):
            _, size, skip = raw_span(k, side)
            halo_rows[side, 0:size] = land[k, side, 0:size].astype(jnp.float32)
            for p in range(orbitals):
                for c in range(2):
                    picked = halo_rows[side, pl.ds(skip + 2 * p + c, REACH, stride=pitch), :]
                    window_lanes = pl.ds(c * LANES, LANES)
                    win[k, p, base : base + REACH, window_lanes] = picked.astype(jnp.bfloat16)

    def second_halo(k, part):
        return halo_copies(1, k, win2, send_r2, part, part * HALF, HALF)

    def fill_window(k, window, to_right, own_rows, tail_rows):
        for p in range(orbitals):
            for c in range(2):
                lanes = pl.ds(c * LANES, LANES)
                (start, stop), at = own_rows, 2 * p + c
                own = rows[k, pl.ds(at + start * pitch, stop - start, stride=pitch), :]
                window[k, p, start:stop, lanes] = own.astype(jnp.bfloat16)
                if to_right is None:
                    continue
                start, stop = tail_rows
                at += (atoms - REACH + start) * pitch
                tail = rows[k, pl.ds(at, stop - start, stride=pitch), :]
                to_right[k, p, start:stop, lanes] = tail.astype(jnp.bfloat16)

    pl.semaphore_wait(barrier, 2 + len(others))
    for k in range(points):
        for copy in first_halo(k):
            copy.start()
    rows[:, atoms * pitch :, :] = jnp.zeros((points, (OWN - atoms) * pitch, LANES), jnp.float32)
    for p in range(WIDE):
        at = (p * PACK + orbitals) * eight
        tiles[at : at + eight, :] = jnp.zeros((eight, LANES), jnp.float32)
    tiles[WIDE * PACK * eight : LANES * eight, :] = jnp.zeros(
        ((LANES - WIDE * PACK) * eight, LANES), jnp.float32
    )
    for p in range(orbitals - WIDE):
        at = (LANES + p * ORB + orbitals) * eight
        tiles[at : at + (ORB - orbitals) * eight, :] = jnp.zeros(
            ((ORB - orbitals) * eight, LANES), jnp.float32
        )

    loads[1].wait()
    for p in range(orbitals):
        for o in range(orbitals):
            at = p * PACK + o if p < WIDE else LANES + (p - WIDE) * ORB + o
            tiles[at * eight : (at + 1) * eight, 0:atoms] = blk[o, p].astype(jnp.float32)
    narrow = LANES // 2
    for s in range(eight):
        wide = tiles[pl.ds(s, LANES, stride=eight), :]
        rest = tiles[pl.ds(LANES * eight + s, narrow, stride=eight), :]
        flat[0, pl.ds(s, atoms, stride=eight), :] = wide.T[:atoms]
        rest = jnp.concatenate([rest, rest], axis=0)
        flat[1, pl.ds(s, atoms, stride=eight), :] = rest.T[:atoms]
    even_side = lax.broadcasted_iota(jnp.int32, (16, LANES), 1) < narrow
    for quad in range(atoms // 4):
        at, to = quad * 32, quad * 48
        gather[z, to : to + 32] = flat[0, at : at + 32].astype(jnp.bfloat16)
        gather[z, to + 32 : to + 48] = jnp.where(
            even_side, flat[1, at : at + 16], flat[1, at + 16 : at + 32]
        ).astype(jnp.bfloat16)
    for c in range(CHUNKS):
        for d, other in enumerate(others):
            block_copy(c, d, z, other).start()
    loads[0].wait()
    for k in range(points):
        own_vectors = vec[k * atoms * pitch : (k + 1) * atoms * pitch]
        rows[k, 0 : atoms * pitch, :] = own_vectors.astype(jnp.float32)
        fill_window(k, win, None, (0, OWN), None)

    spare = pl.ds(RIGHT + REACH, LANES - RIGHT - REACH)
    for window in (win, win2):
        window[:, :, spare, :] = jnp.zeros(
            (points, orbitals, LANES - RIGHT - REACH, 2 * LANES), jnp.bfloat16
        )

    for load in loads[2:]:
        load.wait()
    total = atoms * n_atoms
    row = lax.broadcasted_iota(jnp.int32, (slots, atoms), 1)
    distance = near[...] - (me * atoms + row)
    distance = jnp.where(distance > total // 2, distance - total, distance)
    distance = jnp.where(distance < -(total // 2), distance + total, distance)
    local = row + distance
    place = jnp.where(
        local < 0, local + REACH + LEFT, jnp.where(local >= atoms, local - atoms + RIGHT, local)
    )
    live = lax.broadcasted_iota(jnp.int32, (slots, atoms), 0) < count[...]
    offset = shift[...].astype(jnp.float32)
    grid_row = jnp.floor((offset + 0.5) * (1.0 / 7.0))
    grid_col = offset - 7.0 * grid_row - 3.0
    grid_row = grid_row - 3.0
    columns = [place.astype(jnp.float32)]
    for k in range(points):
        own = lax.broadcasted_iota(jnp.int32, kvecs.shape, 1) == z * points + k
        kvec = jnp.sum(jnp.where(own, kvecs[...], 0.0), axis=1, keepdims=True)
        turns = kvec[0:1] * grid_row + kvec[1:2] * grid_col
        theta = (2.0 * math.pi) * (turns - jnp.floor(turns + 0.5))
        columns += [jnp.where(live, jnp.cos(theta), 0.0), jnp.where(live, jnp.sin(theta), 0.0)]
    for a in range(atoms):
        for j, column in enumerate(columns):
            spread[a, j] = jnp.broadcast_to(column[:, a : a + 1], (slots, LANES))

    lane = lax.broadcasted_iota(jnp.int32, (slots, LANES), 1).astype(jnp.float32)
    depth = 2 * slots
    nothing = jnp.zeros((eight, LANES), jnp.float32)

    def heat(pair, carry):
        for a in range(2):
            atom = 2 * pair + a
            hit = spread[atom, 0] == lane
            for k in range(points):
                for c in range(2):
                    value = jnp.where(hit, spread[atom, 1 + 2 * k + c], 0.0)
                    high = value.astype(jnp.bfloat16).astype(jnp.float32)
                    for part, piece in enumerate((high, value - high)):
                        laid = []
                        for s in range(n_kpt):
                            mine = piece[s * eight : (s + 1) * eight]
                            laid += [nothing, mine] if a else [mine, nothing]
                        hot[atom, k, part * depth : (part + 1) * depth,
                            c * LANES : (c + 1) * LANES] = jnp.concatenate(
                            laid, axis=0
                        ).astype(jnp.bfloat16)
        return carry

    lax.fori_loop(0, pairs, heat, 0, unroll=2)

    def build(quad, carry):
        at = pl.multiple_of(quad * 48, 16)
        for part in range(3):
            held = [gather[s, pl.ds(at + part * 16, 16), :] for s in range(n_kpt)]
            turn[part] = jnp.concatenate(held + held, axis=0).astype(jnp.float32).T
        for pair in range(2):
            stripes = [turn[pair, p * PACK : p * PACK + ORB] for p in range(WIDE)]
            stripes.append(turn[2, pair * narrow : (pair + 1) * narrow])
            flipped = jnp.concatenate(stripes, axis=0).astype(jnp.bfloat16)
            for a in range(2):
                atom = quad * 4 + pair * 2 + a
                for k in range(points):
                    dense = jnp.dot(
                        flipped, hot[atom, k], preferred_element_type=jnp.float32
                    ).astype(jnp.bfloat16)
                    for c in range(2):
                        base = pl.multiple_of(atom * ORB, ORB)
                        for p in range(orbitals):
                            ham[k, c, pl.ds(base, ORB), p * LANES : (p + 1) * LANES] = dense[
                                p * ORB : (p + 1) * ORB, c * LANES : (c + 1) * LANES
                            ]
        return carry

    outs = (first, second)

    def store(step, k):
        return pltpu.make_async_copy(made.at[step, k], outs[step].at[k], store_sem.at[step, k])

    def finish(step, k):
        made[step, k] = rows[k, 0 : atoms * pitch, :].astype(jnp.bfloat16)
        store(step, k).start()

    def apply(k, window, begin, end):
        count_rows = (end - begin) * ORB
        part = ham[k, :, begin * ORB : end * ORB].reshape(2 * count_rows, orbitals * LANES)
        prod[0 : 2 * count_rows] = jnp.dot(
            part,
            window[k].reshape(orbitals * LANES, 2 * LANES),
            preferred_element_type=jnp.float32,
        )
        low, high = slice(0, count_rows), slice(count_rows, 2 * count_rows)
        real = prod[low, 0:LANES] - prod[high, LANES : 2 * LANES]
        imag = prod[low, LANES : 2 * LANES] + prod[high, 0:LANES]
        for c, value in enumerate((real, imag)):
            for a in range(end - begin):
                rows[k, pl.ds((begin + a) * pitch + c, orbitals, stride=2), :] = value[
                    a * ORB : a * ORB + orbitals
                ]

    edges = (0, atoms - HALF, atoms)
    for part in range(2):
        for c in (2 * part, 2 * part + 1):
            for other in others:
                block_copy(c, 0, other, other).wait_recv()
            lax.fori_loop(cuts[c][0], cuts[c][1], build, 0, unroll=True)
        for k in range(points):
            if part == 0:
                for copy in first_halo(k):
                    copy.wait_recv()
                lay_halo(k)
            apply(k, win, edges[part], edges[part + 1])
            own_rows = ((0, HALF), (HALF, OWN))[part]
            fill_window(k, win2, send_r2, own_rows, (part * HALF, (part + 1) * HALF))
            for copy in second_halo(k, part):
                copy.start()
    for k in range(points):
        finish(0, k)
    for k in range(points):
        for part in range(2):
            for copy in second_halo(k, part):
                copy.wait_recv()
        apply(k, win2, 0, atoms)
        finish(1, k)

    for c in range(CHUNKS):
        for d, other in enumerate(others):
            block_copy(c, d, z, other).wait_send()
    for k in range(points):
        for copy in first_halo(k) + second_halo(k, 0) + second_halo(k, 1):
            copy.wait_send()
        for step in range(2):
            store(step, k).wait()


def hand_over(*refs):
    arrays = (len(refs) - 2) // 2
    held, sems = refs[-2], refs[-1]
    pieces = sems.shape[2]
    rows = refs[0].shape[0]
    edges = [i * rows // pieces // 16 * 16 for i in range(pieces)] + [rows]
    steps = []
    for i in range(arrays):
        for j in range(pieces):
            part = pl.ds(edges[j], edges[j + 1] - edges[j])
            here = held.at[i, part]
            fetch = pltpu.make_async_copy(refs[i].at[part], here, sems.at[0, i, j])
            put = pltpu.make_async_copy(here, refs[arrays + i].at[part], sems.at[1, i, j])
            steps.append((fetch, put))
    for fetch, _ in steps:
        fetch.start()
    for fetch, put in steps:
        fetch.wait()
        put.start()
    for _, put in steps:
        put.wait()


def per_device(blocks, vectors, kvecs, neighbours, offsets, counts):
    n_atoms, n_kpt = lax.axis_size("atoms"), lax.axis_size("kpt")
    atoms, eight, orbitals, _ = blocks.shape
    slots = neighbours.shape[1]
    points = vectors.shape[0]
    per_point = (points, atoms * 2 * orbitals, LANES)
    flat_vectors = vectors.transpose(0, 1, 3, 2, 4).reshape(points * per_point[1], LANES)
    landing = -(-(REACH * 2 * orbitals) // HALF) * HALF + HALF
    depth = orbitals * LANES
    bf16, f32 = jnp.bfloat16, jnp.float32
    hbm = pl.BlockSpec(memory_space=pltpu.HBM)
    flops = 2 * points * 2 * 2 * atoms * ORB * depth * 2 * LANES
    args = (
        blocks.transpose(2, 3, 1, 0), flat_vectors, neighbours.T, offsets.T, counts[None, :],
        kvecs.T,
    )
    outs = pl.pallas_call(
        functools.partial(kernel, n_atoms, n_kpt),
        out_shape=[jax.ShapeDtypeStruct(per_point, bf16)] * 2,
        in_specs=[hbm] * len(args),
        out_specs=[hbm] * 2,
        scratch_shapes=[pltpu.VMEM(arg.shape, arg.dtype) for arg in args] + [
            pltpu.VMEM((n_kpt, atoms * eight * 3 // 2, LANES), bf16),
            pltpu.VMEM((points, 2, atoms * ORB, depth), bf16),
            pltpu.VMEM((points, orbitals, LANES, 2 * LANES), bf16),
            pltpu.VMEM((points, orbitals, LANES, 2 * LANES), bf16),
            pltpu.VMEM((points, 2, landing, LANES), bf16),
            pltpu.VMEM((points, orbitals, REACH, 2 * LANES), bf16),
            pltpu.VMEM((points, OWN * 2 * orbitals, LANES), f32),
            pltpu.VMEM((2, landing, LANES), f32),
            pltpu.VMEM((2 * atoms * ORB, 2 * LANES), f32),
            pltpu.VMEM((atoms, points, 4 * slots, 2 * LANES), bf16),
            pltpu.VMEM((atoms, 1 + 2 * points, slots, LANES), f32),
            pltpu.VMEM((LANES * 3 // 2 * eight, LANES), f32),
            pltpu.VMEM((2, atoms * eight, LANES), f32),
            pltpu.VMEM((3, LANES, LANES), f32),
            pltpu.VMEM((2,) + per_point, bf16),
            pltpu.SemaphoreType.DMA((CHUNKS, n_kpt - 1)),
            pltpu.SemaphoreType.DMA((CHUNKS, n_kpt)),
            pltpu.SemaphoreType.DMA((2, points, 2, 2)),
            pltpu.SemaphoreType.DMA((2, points, 2, 2)),
            pltpu.SemaphoreType.DMA((len(args),)),
            pltpu.SemaphoreType.DMA((2, points)),
        ],
        compiler_params=pltpu.CompilerParams(
            collective_id=0, has_side_effects=True, vmem_limit_bytes=60 * 1024 * 1024
        ),
        cost_estimate=pl.CostEstimate(flops=flops, bytes_accessed=4 << 20, transcendentals=0),
    )(*args)
    outs = pl.pallas_call(
        hand_over,
        out_shape=[jax.ShapeDtypeStruct(flat_vectors.shape, bf16)] * 2,
        in_specs=[hbm] * 2,
        out_specs=[hbm] * 2,
        scratch_shapes=[
            pltpu.VMEM((2,) + flat_vectors.shape, bf16),
            pltpu.SemaphoreType.DMA((2, 2, PIECES)),
        ],
        compiler_params=pltpu.CompilerParams(vmem_limit_bytes=60 * 1024 * 1024),
        cost_estimate=pl.CostEstimate(flops=0, bytes_accessed=4 << 20, transcendentals=0),
    )(*(out.reshape(flat_vectors.shape) for out in outs))
    return tuple(
        out.reshape(points, atoms, orbitals, 2, LANES).transpose(0, 1, 3, 2, 4) for out in outs
    )


def solution(mesh):
    placed = (
        P("atoms", "kpt", None, None),
        P("kpt", "atoms", None, None, None),
        P(),
        P("atoms", None),
        P("atoms", None),
        P("atoms"),
    )
    return jax.shard_map(
        per_device,
        mesh=mesh,
        in_specs=placed,
        out_specs=(P("kpt", "atoms", None, None, None), P("kpt", "atoms", None, None, None)),
        check_vma=False,
    )
```
